32 devices in a mesh: section: 4 (over x, core), dp: 8 (over z, y).
Axes of the slice: x: 2, y: 2, z: 4, core: 2. Of those that a mesh axis runs over, the one named last changes fastest.
Arguments:
- latents_in: bfloat16 [2, 8, 256, 384], P(None, 'dp'), may hold values from -6 to 6
- cotangent: bfloat16 [2, 8, 256, 384], P(None, 'dp'), may hold values from -6 to 6
- labels: int32 [2, 8], P(None, 'dp'), may hold values from 0 to 1023
- timesteps: int32 [2, 8], P(None, 'dp'), may hold values from 0 to 1023
- counts: int32 [2, 8], P(None, 'dp'), may hold values from 0 to 1, as said below
- label_table: float32 [1024, 384], replicated, may hold values from -4 to 4
- time_table: float32 [1024, 384], replicated, may hold values from -4 to 4
- adaptive_norm_weight: bfloat16 [4, 384, 2304], P('section', 'dp'), may hold values from -0.3125 to 0.3125
- adaptive_norm_bias: bfloat16 [4, 2304], P('section', 'dp'), may hold values from -3 to 3
- query_key_value_weight: bfloat16 [4, 384, 1152], P('section', 'dp'), may hold values from -0.3125 to 0.3125
- attention_output_weight: bfloat16 [4, 384, 384], P('section', 'dp'), may hold values from -1.25 to 1.25
- up_weight: bfloat16 [4, 384, 1536], P('section', 'dp'), may hold values from -0.3125 to 0.3125
- down_weight: bfloat16 [4, 1536, 384], P('section', 'dp'), may hold values from -0.15625 to 0.15625
Outputs:
- acts: bfloat16 [4, 2, 8, 256, 384], P('section', None, 'dp')
- act_grads: bfloat16 [4, 2, 8, 256, 384], P('section', None, 'dp')
- grad_w_ada: float32 [4, 384, 2304], P('section', 'dp')
- grad_b_ada: float32 [4, 2304], P('section', 'dp')
- grad_w_qkv: float32 [4, 384, 1152], P('section', 'dp')
- grad_w_out: float32 [4, 384, 384], P('section', 'dp')
- grad_w_up: float32 [4, 384, 1536], P('section', 'dp')
- grad_w_down: float32 [4, 1536, 384], P('section', 'dp')
- grad_label_table: float32 [1024, 384], P(('section', 'dp'))
- grad_time_table: float32 [1024, 384], P(('section', 'dp'))
The draws below stay inside these ranges and needn't reach their ends.
Inputs may be any that keep to these rules, and one draw needn't show every extreme that they name: `counts`: in every micro-batch some index of dp holds exactly 1 live latents; the live latents of an index are its first ones; an index may hold none.
All inputs are finite; a program needn't handle non-finite values.
Results may differ from the reference program's by a relative error of at most 0.02.
The reference program's roundings to bfloat16 on the way count: a program that leaves them out, or rounds other values in their place, can miss the bound.
Values may be sent and summed in bfloat16 or wider, within the bound.
No kernel may reach another device: no remote copies, remote signals or barrier semaphores. Data moves between devices by JAX's collectives and lax.ppermute only.
A program may use at most 128 MiB of HBM per device.

```python
import jax
import jax.numpy as jnp
from jax import lax

D = 384
H = 6
HD = 64
FF = 1536
SEQ = 256
CLASSES = 1024
TSTEPS = 1024
MICRO = 2
LAT_DEV = 1
LATENTS = 8
LAYERS = 4
N_SECTION = 4
N_DP = 8


def draw_counts(key, part):
    key = jax.random.fold_in(key, 11)
    first_key, second_key = jax.random.split(key)
    base = jax.random.randint(first_key, (MICRO, N_DP), 0, LAT_DEV + 1)
    filled = jax.random.randint(second_key, (MICRO, 1), 0, N_DP)
    positions = jnp.arange(N_DP, dtype=jnp.int32)[None, :]
    return jnp.where(positions == filled, LAT_DEV, base).astype(jnp.int32)


def place_ends(entries, rng, least, high):
    extent = entries.shape
    place = [jax.random.randint(jax.random.fold_in(rng, axis), (), 0, extent[axis]) for axis in range(len(extent))]
    entries = entries.at[tuple(place)].set(least)
    longest = extent.index(max(extent))
    place[longest] = (place[longest] + 1) % extent[longest]
    return entries.at[tuple(place)].set(high)


def block_scale(stream_key, shape, cuts, low, largest):
    gain, own = 1.0, jax.random.fold_in(stream_key, 6)
    for position, blocks in cuts:
        heights = jnp.exp(jax.random.uniform(jax.random.fold_in(own, position), (blocks,), jnp.float32, low / len(cuts), largest / len(cuts)))
        gain = gain * jnp.repeat(heights, shape[position] // blocks).reshape([-1 if axis == position else 1 for axis in range(len(shape))])
    return gain


def normal_values(key, shape, spread, limit, shards=(), kind=jnp.bfloat16):
    values = spread * jax.random.normal(key, shape, jnp.float32)
    if shards:
        values = values * block_scale(key, shape, shards, -0.22, 0.18)
    return jnp.clip(values, -limit, limit).astype(kind)


def setup_inputs(seed: int = 0) -> dict:
    key_of = jax.random.split(jax.random.key(seed), 14)
    latents_in = normal_values(key_of[0], (MICRO, LATENTS, SEQ, D), 1.0, 6.0, ((1, 8),))
    cotangent = normal_values(key_of[1], (MICRO, LATENTS, SEQ, D), 1.0, 6.0, ((1, 8),))
    labels = place_ends(jax.random.randint(key_of[2], (MICRO, LATENTS), 0, CLASSES), jax.random.fold_in(key_of[2], 1), 0, CLASSES - 1).astype(jnp.int32)
    timesteps = place_ends(jax.random.randint(key_of[3], (MICRO, LATENTS), 0, TSTEPS), jax.random.fold_in(key_of[3], 1), 0, TSTEPS - 1).astype(jnp.int32)
    counts = draw_counts(jax.random.fold_in(key_of[13], 71), 0)
    label_table = normal_values(key_of[5], (CLASSES, D), 0.7, 4.0, (), jnp.float32)
    time_table = normal_values(key_of[6], (TSTEPS, D), 0.7, 4.0, (), jnp.float32)
    adaptive_norm_weight = normal_values(key_of[7], (LAYERS, D, 6 * D), D ** -0.5, 0.3125, ((0, 4), (1, 8)))
    adaptive_norm_bias = normal_values(key_of[8], (LAYERS, 6 * D), 0.5, 3.0, ((0, 4), (1, 8)))
    query_key_value_weight = normal_values(key_of[9], (LAYERS, D, 3 * D), D ** -0.5, 0.3125, ((0, 4), (1, 8)))
    attention_output_weight = normal_values(key_of[10], (LAYERS, D, D), (D // 16) ** -0.5, 1.25, ((0, 4), (1, 8)))
    up_weight = normal_values(key_of[11], (LAYERS, D, FF), D ** -0.5, 0.3125, ((0, 4), (1, 8)))
    down_weight = normal_values(key_of[12], (LAYERS, FF, D), FF ** -0.5, 0.15625, ((0, 4), (1, 8)))
    return {"latents_in": latents_in, "cotangent": cotangent, "labels": labels, "timesteps": timesteps, "counts": counts, "label_table": label_table, "time_table": time_table, "adaptive_norm_weight": adaptive_norm_weight, "adaptive_norm_bias": adaptive_norm_bias, "query_key_value_weight": query_key_value_weight, "attention_output_weight": attention_output_weight, "up_weight": up_weight, "down_weight": down_weight}


epsilon = 1e-06
highest = lax.Precision.HIGHEST

@jax.custom_vjp
def low(v):
    return lax.optimization_barrier(v.astype(jnp.bfloat16)).astype(jnp.float32)

@jax.custom_vjp
def low_back(v):
    return v

def low_keep(v):
    return (low(v), None)

def low_pass(kept, grad):
    return (grad,)

def back_keep(v):
    return (v, None)

def back_low(kept, grad):
    return (low(grad),)
low.defvjp(low_keep, low_pass)
low_back.defvjp(back_keep, back_low)

def normalize(values):
    center = values - lax.optimization_barrier(jnp.mean(values, axis=-1, keepdims=True))
    variance = lax.optimization_barrier(jnp.mean(center * center, axis=-1, keepdims=True))
    return center * lax.rsqrt(variance + epsilon)

def diffusion_transformer_layer(layer_input_rows, conditioning_vector, adaptive_norm_weight, adaptive_norm_bias, query_key_value_weight, attention_output_weight, up_weight, down_weight):
    groups = layer_input_rows.shape[0]
    cond_act = low(jax.nn.silu(conditioning_vector))
    modulate = low_back(jnp.dot(cond_act, adaptive_norm_weight, precision=highest)) + adaptive_norm_bias
    modulate = modulate.reshape(groups, 6, 1, D)
    first_in = low(normalize(layer_input_rows) * (1.0 + modulate[:, 1]) + modulate[:, 0])
    proj_qkv = low_back(low(jnp.einsum('gtd,de->gte', first_in, query_key_value_weight, precision=highest)))
    proj_qkv = proj_qkv.reshape(groups, SEQ, 3, H, HD)
    queries = proj_qkv[:, :, 0]
    keyset = proj_qkv[:, :, 1]
    values = proj_qkv[:, :, 2]
    scores = low_back(jnp.einsum('gqhe,gkhe->ghqk', queries, keyset, precision=highest) * HD ** (-0.5))
    attention = low(jax.nn.softmax(scores, axis=-1))
    mixture = jnp.einsum('ghqk,gkhe->gqhe', attention, values, precision=highest).reshape(groups, SEQ, D)
    mixture = low_back(low(mixture))
    attended = low_back(jnp.einsum('gtd,de->gte', mixture, attention_output_weight, precision=highest))
    middle = layer_input_rows + modulate[:, 2] * attended
    second_in = low(normalize(middle) * (1.0 + modulate[:, 4]) + modulate[:, 3])
    hidden = low_back(jnp.einsum('gtd,df->gtf', second_in, up_weight, precision=highest))
    activated = low(jax.nn.gelu(hidden, approximate=True))
    result = low_back(jnp.einsum('gtf,fd->gtd', activated, down_weight, precision=highest))
    return middle + modulate[:, 5] * result

def stack_forward(probes, label_table, time_table, adaptive_norm_weight, adaptive_norm_bias, query_key_value_weight, attention_output_weight, up_weight, down_weight, start_rows, label_ids, time_ids, living_token_rows):
    conditioning_vector = label_table[label_ids] + time_table[time_ids]
    current = start_rows
    outputs = []
    for current_layer_index in range(N_SECTION):
        incoming_state = low_back(current + probes[current_layer_index])
        emitted_state = diffusion_transformer_layer(incoming_state, conditioning_vector, adaptive_norm_weight[current_layer_index], adaptive_norm_bias[current_layer_index], query_key_value_weight[current_layer_index], attention_output_weight[current_layer_index], up_weight[current_layer_index], down_weight[current_layer_index]) * living_token_rows[:, None, None]
        current = low(emitted_state)
        outputs.append(current)
    return (current, jnp.stack(outputs))

def reference(latents_in, cotangent, labels, timesteps, counts, label_table, time_table, adaptive_norm_weight, adaptive_norm_bias, query_key_value_weight, attention_output_weight, up_weight, down_weight):
    weight_list = (adaptive_norm_weight.astype(jnp.float32), adaptive_norm_bias.astype(jnp.float32), query_key_value_weight.astype(jnp.float32), attention_output_weight.astype(jnp.float32), up_weight.astype(jnp.float32), down_weight.astype(jnp.float32))
    group_count = MICRO * N_DP
    starts = latents_in.astype(jnp.float32).reshape(group_count, LAT_DEV, SEQ, D)
    cotans = cotangent.astype(jnp.float32).reshape(group_count, LAT_DEV, SEQ, D)
    label_groups = labels.reshape(group_count, LAT_DEV)
    time_groups = timesteps.reshape(group_count, LAT_DEV)
    alive_all = (jnp.arange(LAT_DEV, dtype=jnp.int32)[None, None, :] < counts[:, :, None]).astype(jnp.float32)
    alive_all = alive_all.reshape(group_count, LAT_DEV)
    zero_probes = jnp.zeros((N_SECTION, LAT_DEV, SEQ, D), jnp.float32)

    def accumulate(totals, pieces):
        start_rows, cot_rows, label_ids, time_ids, living_token_rows = pieces

        def wrapped(probes, label_tab, time_tab, wa_all, ba_all, wq_all, wo_all, wu_all, wd_all):
            return stack_forward(probes, label_tab, time_tab, wa_all, ba_all, wq_all, wo_all, wu_all, wd_all, start_rows, label_ids, time_ids, living_token_rows)
        final_out, pullback, stacked = jax.vjp(wrapped, zero_probes, label_table, time_table, weight_list[0], weight_list[1], weight_list[2], weight_list[3], weight_list[4], weight_list[5], has_aux=True)
        gradients = pullback(cot_rows)
        totals = jax.tree.map(lambda earlier, latest: earlier + latest, totals, tuple(gradients[1:]))
        return (totals, (stacked, gradients[0]))
    initial = (jnp.zeros_like(label_table), jnp.zeros_like(time_table)) + tuple((jnp.zeros_like(w) for w in weight_list))
    totals, (stacked, entry_grads) = lax.scan(accumulate, initial, (starts, cotans, label_groups, time_groups, alive_all))

    def arrange(blocks):
        blocks = blocks.reshape(MICRO, N_DP, N_SECTION, LAT_DEV, SEQ, D).transpose(2, 0, 1, 3, 4, 5)
        return blocks.reshape(N_SECTION, MICRO, N_DP * LAT_DEV, SEQ, D).astype(jnp.bfloat16)
    return (arrange(stacked), arrange(entry_grads), totals[2], totals[3], totals[4], totals[5], totals[6], totals[7], totals[0], totals[1])
```

```python
from functools import partial

import jax
import jax.numpy as jnp
from jax import lax
from jax.experimental import pallas as pl
from jax.experimental.pallas import tpu as pltpu
from jax.sharding import Mesh, PartitionSpec as P

D = 384
H = 6
HD = 64
FF = 1536
SEQ = 256
CLASSES = 1024
MICRO = 2
BLOCKS = 12
CHUNKS = FF // D
PAIR = 2 * HD

epsilon = 1e-06
highest = lax.Precision.HIGHEST
f32 = jnp.float32
bf16 = jnp.bfloat16
VMEM_BYTES = 56 * 1024 * 1024


def dot(a, b):
    return lax.dot_general(a, b, (((1,), (0,)), ((), ())), preferred_element_type=f32)


def dot_nt(a, b):
    return lax.dot_general(a, b, (((1,), (1,)), ((), ())), preferred_element_type=f32)


def dot_tn(a, b):
    return lax.dot_general(a, b, (((0,), (0,)), ((), ())), preferred_element_type=f32)


def normalize(values):
    center = values - jnp.mean(values, axis=-1, keepdims=True)
    inverse = lax.rsqrt(jnp.mean(center * center, axis=-1, keepdims=True) + epsilon)
    return center * inverse, inverse


def norm_back(upstream, normed, inverse):
    return inverse * (
        upstream
        - jnp.mean(upstream, axis=-1, keepdims=True)
        - normed * jnp.mean(upstream * normed, axis=-1, keepdims=True)
    )


def token_sum(values):
    return jnp.sum(values, axis=0, keepdims=True)


def half_masks():
    lane = lax.broadcasted_iota(jnp.int32, (SEQ, PAIR), 1)
    return lane < HD


def forward_layer(z, mod, alive, wa, wd, saved):
    row = lambda i: mod[i : i + 1, :]
    normed, _ = normalize(z)
    first_in = (normed * (1.0 + row(1)) + row(0)).astype(bf16)
    parts = [dot(first_in, wa[j]).astype(bf16) for j in range(3)]
    for j in range(3):
        saved["qkv"][:, j * D : (j + 1) * D] = parts[j]
    low_half = half_masks()
    mixed = []
    for pair in range(H // 2):
        cols = slice(pair * PAIR, (pair + 1) * PAIR)
        q, k, v = (part[:, cols] for part in parts)
        outs = []
        for e in range(2):
            mask = low_half if e == 0 else jnp.logical_not(low_half)
            q_e = jnp.where(mask, q * HD ** (-0.5), 0).astype(bf16)
            scores = dot_nt(q_e, k)
            grown = jnp.exp(scores - jnp.max(scores, axis=-1, keepdims=True))
            probs = (grown / jnp.sum(grown, axis=-1, keepdims=True)).astype(bf16)
            saved["probs"][pair * 2 + e] = probs
            outs.append(dot(probs, v))
        mixed.append(jnp.where(low_half, outs[0], outs[1]).astype(bf16))
    mixture = jnp.concatenate(mixed, axis=1)
    saved["mixture"][...] = mixture
    attended = dot(mixture, wa[3])
    saved["attended"][...] = attended
    middle = z + row(2) * attended
    normed_two, _ = normalize(middle)
    second_in = (normed_two * (1.0 + row(4)) + row(3)).astype(bf16)
    result = jnp.zeros((SEQ, D), f32)
    c0 = (2.0 / jnp.pi) ** 0.5
    for c in range(CHUNKS):
        cols = slice(c * D, (c + 1) * D)
        hidden = dot(second_in, wa[4 + c])
        square = hidden * hidden
        tanh = jnp.tanh(c0 * hidden * (1.0 + 0.044715 * square))
        half = 0.5 * (1.0 + tanh)
        slope = half + 0.5 * hidden * (1.0 - tanh * tanh) * (c0 * (1.0 + 3 * 0.044715 * square))
        activated = (hidden * half).astype(bf16)
        saved["activated"][:, cols] = activated
        saved["slope"][:, cols] = slope.astype(bf16)
        result = result + dot(activated, wd(c))
    saved["result"][...] = result
    return (middle + row(5) * result) * alive


def backward_mlp(grad_out, z, mod, alive, wa, wd, saved, pack=None):
    row = lambda i: mod[i : i + 1, :]
    attended = saved["attended"][...]
    middle = z + row(2) * attended
    normed_two, inverse_two = normalize(middle)
    grad_y = grad_out * alive
    grad_gate_m = token_sum(grad_y * saved["result"][...])
    grad_result = (row(5) * grad_y).astype(bf16)
    grad_second = jnp.zeros((SEQ, D), f32)
    if pack is not None:
        pack[:, 0:D] = (normed_two * (1.0 + row(4)) + row(3)).astype(bf16)
        pack[:, D : 2 * D] = grad_result
    for c in range(CHUNKS):
        cols = slice(c * D, (c + 1) * D)
        grad_act = dot_nt(grad_result, wd(c))
        grad_hidden = (grad_act * saved["slope"][:, cols].astype(f32)).astype(bf16)
        if pack is not None:
            pack[:, 2 * D + c * D : 2 * D + (c + 1) * D] = grad_hidden
            pack[:, 6 * D + c * D : 6 * D + (c + 1) * D] = saved["activated"][:, cols]
        grad_second = grad_second + dot_nt(grad_hidden, wa[4 + c])
    grad_scale_m = token_sum(grad_second * normed_two)
    grad_shift_m = token_sum(grad_second)
    grad_middle = grad_y + norm_back(grad_second * (1.0 + row(4)), normed_two, inverse_two)
    grad_gate_a = token_sum(grad_middle * attended)
    return grad_middle, (grad_gate_a, grad_shift_m, grad_scale_m, grad_gate_m)


def backward_attention(grad_middle, z, mod, wa, saved, pack=None):
    row = lambda i: mod[i : i + 1, :]
    normed, inverse = normalize(z)
    grad_attended = (row(2) * grad_middle).astype(bf16)
    grad_mixture = dot_nt(grad_attended, wa[3]).astype(bf16)
    low_half = half_masks()
    grads = [[], [], []]
    zero = jnp.zeros((SEQ, PAIR), bf16)
    for pair in range(H // 2):
        cols = [slice(j * D + pair * PAIR, j * D + (pair + 1) * PAIR) for j in range(3)]
        q, k, v = (saved["qkv"][:, c] for c in cols)
        grad_mix = grad_mixture[:, pair * PAIR : (pair + 1) * PAIR]
        outs = []
        for e in range(2):
            mask = low_half if e == 0 else jnp.logical_not(low_half)
            probs = saved["probs"][pair * 2 + e]
            grad_probs = dot_nt(jnp.where(mask, grad_mix, zero), v)
            wide = probs.astype(f32)
            weighted = grad_probs * wide
            grad_scores = (weighted - wide * jnp.sum(weighted, axis=-1, keepdims=True)).astype(bf16)
            outs.append(
                (
                    dot(grad_scores, k) * HD ** (-0.5),
                    dot_tn(grad_scores, q) * HD ** (-0.5),
                    dot_tn(probs, grad_mix),
                )
            )
        for j in range(3):
            grads[j].append(jnp.where(low_half, outs[0][j], outs[1][j]).astype(bf16))
    grads = [jnp.concatenate(g, axis=1) for g in grads]
    grad_first = dot_nt(grads[0], wa[0]) + dot_nt(grads[1], wa[1]) + dot_nt(grads[2], wa[2])
    if pack is not None:
        pack[:, 0:D] = (normed * (1.0 + row(1)) + row(0)).astype(bf16)
        for j in range(3):
            pack[:, D + j * D : 2 * D + j * D] = grads[j]
        pack[:, 4 * D : 5 * D] = saved["mixture"][...]
        pack[:, 5 * D : 6 * D] = grad_attended
    grad_scale_a = token_sum(grad_first * normed)
    grad_shift_a = token_sum(grad_first)
    grad_in = grad_middle + norm_back(grad_first * (1.0 + row(1)), normed, inverse)
    return grad_in, (grad_shift_a, grad_scale_a)


SAVED = (
    ("qkv", (SEQ, 3 * D), bf16),
    ("probs", (H, SEQ, SEQ), bf16),
    ("mixture", (SEQ, D), bf16),
    ("attended", (SEQ, D), f32),
    ("activated", (SEQ, FF), bf16),
    ("slope", (SEQ, FF), bf16),
    ("result", (SEQ, D), f32),
)
NAMES = tuple(name for name, _, _ in SAVED)


def weight_copies(scalars, own, other, layer, wa, wd, sem):
    pieces = len(own)
    rows = D // pieces
    dp = scalars[0]
    mine = scalars[2] == layer

    def make(source, k):
        place = jnp.bitwise_xor(dp, k) if pieces > 1 else 0
        start = pl.multiple_of(place * rows, 16)
        first = pltpu.make_async_copy(
            source[k].at[pl.ds(0, 8)], wa.at[:, pl.ds(start, rows), :], sem.at[0, k]
        )
        second = pltpu.make_async_copy(
            source[k].at[pl.ds(8, 4)], wd.at[pl.ds(place * 4, 4)], sem.at[1, k]
        )
        return first, second

    def start():
        for source, chosen in ((own, mine), (other, jnp.logical_not(mine))):

            @pl.when(chosen)
            def _():
                for k in range(pieces):
                    for copy in make(source, k):
                        copy.start()

    def wait():
        for k in range(pieces):
            for copy in make(own, k):
                copy.wait()

    return start, wait


def down_chunk(wd_ref):
    blocks = wd_ref.shape[0]
    per = blocks // CHUNKS
    rows = wd_ref.shape[1]

    def chunk(c):
        return wd_ref[c * per : (c + 1) * per].reshape(per * rows, D)

    return chunk


def forward_kernel(pieces, scalars, latents, arriving, mods, *refs):
    own, other = refs[:pieces], refs[pieces : 2 * pieces]
    rest = refs[2 * pieces :]
    outs = rest[:2]
    saved = [dict(zip(NAMES, rest[2 + 7 * layer : 9 + 7 * layer])) for layer in range(2)]
    wa, wd, sems = rest[16:]
    handles = [
        weight_copies(scalars, own, other, layer, wa.at[layer], wd.at[layer], sems.at[layer])
        for layer in range(2)
    ]
    for start, _ in handles:
        start()
    alive = jnp.where(scalars[3] > 0, 1.0, 0.0).astype(f32)
    z = jnp.where(scalars[1] == 0, latents[scalars[2]], arriving[...])
    for layer in range(2):
        handles[layer][1]()
        z = forward_layer(
            z.astype(f32),
            mods[layer],
            alive,
            wa.at[layer],
            down_chunk(wd.at[layer]),
            saved[layer],
        ).astype(bf16)
        outs[layer][...] = z


def weight_scratch(pieces, layers):
    rows = D // pieces
    return [
        pltpu.VMEM((layers, 8, D, D), bf16),
        pltpu.VMEM((layers, 4 * pieces, rows, D), bf16),
        pltpu.SemaphoreType.DMA((layers, 2, pieces)),
    ]


vmem = pl.BlockSpec(memory_space=pltpu.VMEM)
smem = pl.BlockSpec(memory_space=pltpu.SMEM)
hbm = pl.BlockSpec(memory_space=pl.ANY)


def run_forward(scalars, latents, arriving, mods, own, other):
    pieces = len(own)
    shapes = [jax.ShapeDtypeStruct((SEQ, D), bf16)] * 2
    shapes += [jax.ShapeDtypeStruct(shape, kind) for _, shape, kind in SAVED] * 2
    out = pl.pallas_call(
        partial(forward_kernel, pieces),
        out_shape=shapes,
        in_specs=[smem, vmem, vmem, vmem] + [hbm] * (2 * pieces),
        out_specs=[vmem] * len(shapes),
        scratch_shapes=weight_scratch(pieces, 2),
        compiler_params=pltpu.CompilerParams(vmem_limit_bytes=VMEM_BYTES),
        name="forward",
    )(scalars, latents, arriving, mods, *own, *other)
    return out[0], out[1], out[2:9], out[9:16]


def backward_kernel(pieces, layer, keep, scalars, grads, grad_in, z_in, mods, *refs):
    own, other = refs[:pieces], refs[pieces : 2 * pieces]
    rest = refs[2 * pieces :]
    saved = dict(zip(NAMES, rest[:7]))
    rest = rest[7:]
    if keep:
        out, grad_mod, pack_m, pack_a = rest[:4]
        rest = rest[4:]
    else:
        out, pack_m, pack_a = rest[0], None, None
        rest = rest[1:]
    wa, wd, sems = rest
    start, wait = weight_copies(scalars, own, other, layer, wa.at[0], wd.at[0], sems.at[0])
    start()
    alive = jnp.where(scalars[3] > 0, 1.0, 0.0).astype(f32)
    if layer == 1:
        upstream = jnp.where(scalars[1] == 1, grads[scalars[2]], grad_in[...])
    else:
        upstream = grad_in[...]
    z = z_in[...].astype(f32) if layer == 1 else jnp.where(
        scalars[1] == 0, grads[scalars[2]], z_in[...]
    ).astype(f32)
    mod = mods[layer]
    wait()
    grad_middle, four = backward_mlp(
        upstream.astype(f32), z, mod, alive, wa.at[0], down_chunk(wd.at[0]), saved, pack_m
    )
    grad_z, two = backward_attention(grad_middle, z, mod, wa.at[0], saved, pack_a)
    out[...] = grad_z.astype(bf16)
    if keep:
        grad_mod[...] = jnp.concatenate(two + four, axis=0)


def run_backward(layer, keep, scalars, grads, grad_in, z_in, mods, own, other, saved):
    pieces = len(own)
    shapes = [jax.ShapeDtypeStruct((SEQ, D), bf16)]
    if keep:
        shapes += [
            jax.ShapeDtypeStruct((6, D), f32),
            jax.ShapeDtypeStruct((SEQ, 10 * D), bf16),
            jax.ShapeDtypeStruct((SEQ, 6 * D), bf16),
        ]
    return pl.pallas_call(
        partial(backward_kernel, pieces, layer, keep),
        out_shape=shapes,
        in_specs=[smem, vmem, vmem, vmem, vmem] + [hbm] * (2 * pieces) + [vmem] * 7,
        out_specs=[vmem] * len(shapes),
        scratch_shapes=weight_scratch(pieces, 1),
        compiler_params=pltpu.CompilerParams(vmem_limit_bytes=VMEM_BYTES),
        name="backward",
    )(scalars, grads, grad_in, z_in, mods, *own, *other, *saved)


def weight_grad_kernel(pieces, layer, scalars, pack_m, got_m, pack_a, got_a, *refs):
    outs, (block, tall) = refs[:pieces], refs[pieces:]
    rows = D // pieces
    dp = scalars[0]

    def places(k):
        return jnp.bitwise_xor(dp, k) if pieces > 1 else 0

    @pl.when(scalars[2] == layer)
    def _():
        def product(own, got, a, b):
            left, right = slice(a * D, (a + 1) * D), slice(b * D, (b + 1) * D)
            return (
                dot_tn(own[:, left], own[:, right]) + dot_tn(got[:, left], got[:, right])
            ).astype(bf16)

        pairs = [(pack_a, got_a, 0, 1 + j) for j in range(3)]
        pairs += [(pack_a, got_a, 4, 5)]
        pairs += [(pack_m, got_m, 0, 2 + c) for c in range(4)]
        for j, pair in enumerate(pairs):
            block[j] = product(*pair)
        for c in range(CHUNKS):
            tall[c * D : (c + 1) * D, :] = product(pack_m, got_m, 6 + c, 1)
        for k in range(pieces):
            start = pl.multiple_of(places(k) * rows, 16)
            outs[k][0:8] = block[:, pl.ds(start, rows), :]
            start = pl.multiple_of(places(k) * 4 * rows, 16)
            outs[k][8:12] = tall[pl.ds(start, 4 * rows), :].reshape(4, rows, D)

    @pl.when(scalars[2] != layer)
    def _():
        for k in range(pieces):
            outs[k][...] = jnp.zeros_like(outs[k])


def run_weight_grad(pieces, layer, scalars, pack_m, got_m, pack_a, got_a):
    rows = D // pieces
    return pl.pallas_call(
        partial(weight_grad_kernel, pieces, layer),
        out_shape=[jax.ShapeDtypeStruct((BLOCKS, rows, D), bf16)] * pieces,
        in_specs=[smem] + [vmem] * 4,
        out_specs=[vmem] * pieces,
        scratch_shapes=[pltpu.VMEM((8, D, D), bf16), pltpu.VMEM((FF, D), bf16)],
        compiler_params=pltpu.CompilerParams(vmem_limit_bytes=VMEM_BYTES),
        name="weight_grad",
    )(scalars, pack_m, got_m, pack_a, got_a)


def swap(value, axis, bit):
    count = lax.axis_size(axis)
    return lax.ppermute(value, axis, [(i, i ^ bit) for i in range(count)])


def one_way(value, axis, source, target):
    return lax.ppermute(value, axis, [(source, target)])


def doubling_gather(value, axis):
    count = lax.axis_size(axis)
    value = value[None]
    bit = 1
    while bit < count:
        value = jnp.concatenate([value, swap(value, axis, bit)], axis=0)
        bit *= 2
    return value


def halving_scatter(value, axis):
    bit = lax.axis_size(axis) // 2
    while bit >= 1:
        value = value[:bit] + swap(value[bit:], axis, bit)
        bit //= 2
    return value[0]


def gather_pieces(shard):
    pieces = [shard] + [swap(shard, "dp", 2 * k) for k in range(1, 4)]
    across = [swap(piece, "dp", 1) for piece in pieces]
    return [piece for both in zip(pieces, across) for piece in both]


def scatter_pieces(parts):
    across = [swap(parts[2 * k + 1], "dp", 1) for k in (3, 2, 1, 0)][::-1]
    sums = [parts[2 * k].astype(f32) + across[k].astype(f32) for k in range(4)]
    far = [swap(sums[k].astype(bf16), "dp", 2 * k) for k in (3, 2, 1)]
    total = sums[0]
    for piece in far:
        total = total + piece.astype(f32)
    return total


def local(
    latents_in,
    cotangent,
    labels,
    timesteps,
    counts,
    label_table,
    time_table,
    adaptive_norm_weight,
    adaptive_norm_bias,
    query_key_value_weight,
    attention_output_weight,
    up_weight,
    down_weight,
):
    dp_count = lax.axis_size("dp")
    dp, x, core = (lax.axis_index(name) for name in ("dp", "x", "core"))
    rows = D // dp_count
    small = dp_count == 8
    latents = latents_in[:, 0]
    cotangents = cotangent[:, 0]
    live = jnp.where(core == 0, counts[0, 0], counts[1, 0])
    scalars = jnp.stack([dp, x, core, live]).astype(jnp.int32)

    blocks = jnp.concatenate(
        [
            query_key_value_weight[0].reshape(rows, 3, D).transpose(1, 0, 2),
            attention_output_weight[0][None],
            up_weight[0].reshape(rows, CHUNKS, D).transpose(1, 0, 2),
        ],
        axis=0,
    )
    if small:
        shard = jnp.concatenate([blocks, down_weight[0].reshape(CHUNKS, rows, D)], axis=0)
        own = gather_pieces(shard)
    else:
        own = [
            jnp.concatenate(
                [
                    lax.all_gather(blocks, "dp", axis=1, tiled=True),
                    lax.all_gather(down_weight[0], "dp", axis=0, tiled=True).reshape(CHUNKS, D, D),
                ],
                axis=0,
            )
        ]
    pieces = len(own)
    other = [swap(piece, "core", 1) for piece in own]

    ids = jnp.stack([labels[:, 0], timesteps[:, 0]])
    ids = doubling_gather(ids, "dp")
    condition = label_table[ids[:, 0]] + time_table[ids[:, 1]]
    condition = lax.dynamic_slice_in_dim(condition, dp * rows, rows, axis=2)
    condition = condition.reshape(dp_count * MICRO, rows)
    cond_act = jax.nn.silu(condition).astype(bf16)
    ada = adaptive_norm_weight[0]
    width = 6 * D // dp_count
    bias = lax.dynamic_update_slice_in_dim(
        jnp.zeros((6 * D,), f32), adaptive_norm_bias[0].astype(f32), dp * width, 0
    )
    linear = jnp.dot(cond_act, ada, preferred_element_type=f32) + bias
    linear = halving_scatter(linear.reshape(dp_count, MICRO, 6 * D), "dp")
    mine = jnp.where(core == 0, linear[0], linear[1])
    theirs = swap(jnp.where(core == 0, linear[1], linear[0]), "core", 1)
    mods = jnp.where(core == 0, jnp.stack([mine, theirs]), jnp.stack([theirs, mine]))
    mods = mods.reshape(2, 6, D)

    arriving = jnp.zeros((SEQ, D), bf16)
    _, leaving, _, _ = run_forward(scalars, latents, arriving, mods, own, other)
    arriving = one_way(leaving, "x", 0, 1)
    act_a, act_b, saved_a, saved_b = run_forward(scalars, latents, arriving, mods, own, other)

    def back(layer, keep, grad_in):
        if layer == 1:
            args = (cotangents, grad_in, act_a)
            saved = saved_b
        else:
            args = (latents, grad_in, arriving)
            saved = saved_a
        return run_backward(layer, keep, scalars, *args, mods, own, other, saved)

    grad_in = jnp.zeros((SEQ, D), bf16)
    (grad_b,) = back(1, False, grad_in)
    (grad_a,) = back(0, False, grad_b)
    grad_in = one_way(grad_a, "x", 1, 0)
    grad_b, mod_b, pack_m_b, pack_a_b = back(1, True, grad_in)
    grad_a, mod_a, pack_m_a, pack_a_a = back(0, True, grad_b)

    def weight_grads(layer, pack_m, pack_a):
        got_m = one_way(pack_m, "core", 1 - layer, layer)
        got_a = one_way(pack_a, "core", 1 - layer, layer)
        parts = run_weight_grad(pieces, layer, scalars, pack_m, got_m, pack_a, got_a)
        if small:
            return scatter_pieces(parts)
        square = lax.psum_scatter(
            parts[0][:8].astype(f32), "dp", scatter_dimension=1, tiled=True
        )
        tall = lax.psum_scatter(
            parts[0][8:].astype(f32).reshape(FF, D), "dp", scatter_dimension=0, tiled=True
        )
        return jnp.concatenate([square, tall.reshape(CHUNKS, rows, D)], axis=0)

    total_b = weight_grads(1, pack_m_b, pack_a_b)
    total_a = weight_grads(0, pack_m_a, pack_a_a)
    total = jnp.where(core == 0, total_a, total_b)
    grad_w_qkv = total[0:3].transpose(1, 0, 2).reshape(rows, 3 * D)
    grad_w_out = total[3]
    grad_w_up = total[4:8].transpose(1, 0, 2).reshape(rows, FF)
    grad_w_down = total[8:12].reshape(CHUNKS * rows, D)

    def both_micros(first, second):
        mine = jnp.where(core == 0, first, second)
        theirs = swap(jnp.where(core == 0, second, first), "core", 1)
        return jnp.where(core == 0, jnp.stack([mine, theirs]), jnp.stack([theirs, mine]))

    acts = both_micros(act_a, act_b)
    act_grads = both_micros(grad_a, grad_b)

    grad_mod = both_micros(mod_a.reshape(6 * D), mod_b.reshape(6 * D))
    grad_mod = doubling_gather(grad_mod, "dp").reshape(dp_count * MICRO, 6 * D)
    grad_mod_low = grad_mod.astype(bf16)
    grad_w_ada = jnp.dot(cond_act.T, grad_mod_low, preferred_element_type=f32)
    grad_b_ada = lax.dynamic_slice_in_dim(jnp.sum(grad_mod, axis=0), dp * width, width)
    _, silu_pull = jax.vjp(jax.nn.silu, condition)
    grad_cond = silu_pull(
        lax.dot_general(grad_mod_low, ada, (((1,), (1,)), ((), ())), preferred_element_type=f32)
    )[0]
    grad_cond = grad_cond + swap(grad_cond, "core", 1)
    grad_cond = grad_cond + swap(grad_cond, "x", 1)
    gathered = grad_cond.reshape(1, dp_count, MICRO, rows)
    bit = 1
    while bit < dp_count:
        got = swap(gathered, "dp", bit)
        split = got.reshape(bit, dp_count // (2 * bit), 2, bit, MICRO, rows)
        got = jnp.flip(split, axis=2).reshape(gathered.shape)
        gathered = jnp.concatenate([gathered, got], axis=0)
        bit *= 2
    order = jnp.bitwise_xor(jnp.arange(dp_count, dtype=jnp.int32), dp)
    table_rows = jnp.take(gathered, order, axis=0)
    table_rows = table_rows.transpose(1, 2, 0, 3).reshape(dp_count * MICRO, D)
    share = CLASSES // (4 * dp_count)
    base = ((x * 2 + core) * dp_count + dp) * share
    targets = base + jnp.arange(share, dtype=jnp.int32)
    label_hot = (targets[:, None] == ids[:, 0].reshape(1, -1)).astype(f32)
    time_hot = (targets[:, None] == ids[:, 1].reshape(1, -1)).astype(f32)
    label_part = jnp.dot(label_hot, table_rows, precision=highest)
    time_part = jnp.dot(time_hot, table_rows, precision=highest)

    return (
        acts[None, :, None],
        act_grads[None, :, None],
        grad_w_ada[None],
        grad_b_ada[None],
        grad_w_qkv[None],
        grad_w_out[None],
        grad_w_up[None],
        grad_w_down[None],
        label_part,
        time_part,
    )


def solution(mesh):
    sections, dp_count = mesh.devices.shape
    grid = Mesh(mesh.devices.reshape(2, sections // 2, dp_count), ("x", "core", "dp"))
    section = ("x", "core")
    return jax.shard_map(
        local,
        mesh=grid,
        in_specs=(
            P(None, "dp", None, None),
            P(None, "dp", None, None),
            P(None, "dp"),
            P(None, "dp"),
            P(None, "dp"),
            P(),
            P(),
            P(section, "dp", None),
            P(section, "dp"),
            P(section, "dp", None),
            P(section, "dp", None),
            P(section, "dp", None),
            P(section, "dp", None),
        ),
        out_specs=(
            P(section, None, "dp", None, None),
            P(section, None, "dp", None, None),
            P(section, "dp", None),
            P(section, "dp"),
            P(section, "dp", None),
            P(section, "dp", None),
            P(section, "dp", None),
            P(section, "dp", None),
            P(("x", "core", "dp"), None),
            P(("x", "core", "dp"), None),
        ),
        check_vma=False,
    )
```

```python
from functools import partial

import jax
import jax.numpy as jnp
from jax import lax
from jax.experimental import pallas as pl
from jax.experimental.pallas import tpu as pltpu
from jax.sharding import Mesh, PartitionSpec as P

D = 384
H = 6
HD = 64
FF = 1536
SEQ = 256
CLASSES = 1024
MICRO = 2
BLOCKS = 12
CHUNKS = FF // D
PAIR = 2 * HD

epsilon = 1e-06
highest = lax.Precision.HIGHEST
f32 = jnp.float32
bf16 = jnp.bfloat16
VMEM_BYTES = 56 * 1024 * 1024


def dot(a, b):
    return lax.dot_general(a, b, (((1,), (0,)), ((), ())), preferred_element_type=f32)


def dot_nt(a, b):
    return lax.dot_general(a, b, (((1,), (1,)), ((), ())), preferred_element_type=f32)


def dot_tn(a, b):
    return lax.dot_general(a, b, (((0,), (0,)), ((), ())), preferred_element_type=f32)


def normalize(values):
    center = values - jnp.mean(values, axis=-1, keepdims=True)
    inverse = lax.rsqrt(jnp.mean(center * center, axis=-1, keepdims=True) + epsilon)
    return center * inverse, inverse


def norm_back(upstream, normed, inverse):
    return inverse * (
        upstream
        - jnp.mean(upstream, axis=-1, keepdims=True)
        - normed * jnp.mean(upstream * normed, axis=-1, keepdims=True)
    )


def token_sum(values):
    return jnp.sum(values, axis=0, keepdims=True)


def half_masks():
    lane = lax.broadcasted_iota(jnp.int32, (SEQ, PAIR), 1)
    return lane < HD


def forward_layer(z, mod, alive, wa, wd, saved):
    row = lambda i: mod[i : i + 1, :]
    normed, _ = normalize(z)
    first_in = (normed * (1.0 + row(1)) + row(0)).astype(bf16)
    parts = [dot(first_in, wa[j]).astype(bf16) for j in range(3)]
    for j in range(3):
        saved["qkv"][:, j * D : (j + 1) * D] = parts[j]
    low_half = half_masks()
    mixed = []
    for pair in range(H // 2):
        cols = slice(pair * PAIR, (pair + 1) * PAIR)
        q, k, v = (part[:, cols] for part in parts)
        outs = []
        for e in range(2):
            mask = low_half if e == 0 else jnp.logical_not(low_half)
            q_e = jnp.where(mask, q * HD ** (-0.5), 0).astype(bf16)
            scores = dot_nt(q_e, k)
            grown = jnp.exp(scores - jnp.max(scores, axis=-1, keepdims=True))
            probs = (grown / jnp.sum(grown, axis=-1, keepdims=True)).astype(bf16)
            saved["probs"][pair * 2 + e] = probs
            outs.append(dot(probs, v))
        mixed.append(jnp.where(low_half, outs[0], outs[1]).astype(bf16))
    mixture = jnp.concatenate(mixed, axis=1)
    saved["mixture"][...] = mixture
    attended = dot(mixture, wa[3])
    saved["attended"][...] = attended
    middle = z + row(2) * attended
    normed_two, _ = normalize(middle)
    second_in = (normed_two * (1.0 + row(4)) + row(3)).astype(bf16)
    result = jnp.zeros((SEQ, D), f32)
    c0 = (2.0 / jnp.pi) ** 0.5
    for c in range(CHUNKS):
        cols = slice(c * D, (c + 1) * D)
        hidden = dot(second_in, wa[4 + c])
        square = hidden * hidden
        tanh = jnp.tanh(c0 * hidden * (1.0 + 0.044715 * square))
        half = 0.5 * (1.0 + tanh)
        slope = half + 0.5 * hidden * (1.0 - tanh * tanh) * (c0 * (1.0 + 3 * 0.044715 * square))
        activated = (hidden * half).astype(bf16)
        saved["activated"][:, cols] = activated
        saved["slope"][:, cols] = slope.astype(bf16)
        result = result + dot(activated, wd(c))
    saved["result"][...] = result
    return (middle + row(5) * result) * alive


def backward_mlp(grad_out, z, mod, alive, wa, wd, saved, pack=None):
    row = lambda i: mod[i : i + 1, :]
    attended = saved["attended"][...]
    middle = z + row(2) * attended
    normed_two, inverse_two = normalize(middle)
    grad_y = grad_out * alive
    grad_gate_m = token_sum(grad_y * saved["result"][...])
    grad_result = (row(5) * grad_y).astype(bf16)
    grad_second = jnp.zeros((SEQ, D), f32)
    if pack is not None:
        pack[:, 0:D] = (normed_two * (1.0 + row(4)) + row(3)).astype(bf16)
        pack[:, D : 2 * D] = grad_result
    for c in range(CHUNKS):
        cols = slice(c * D, (c + 1) * D)
        grad_act = dot_nt(grad_result, wd(c))
        grad_hidden = (grad_act * saved["slope"][:, cols].astype(f32)).astype(bf16)
        if pack is not None:
            pack[:, 2 * D + c * D : 2 * D + (c + 1) * D] = grad_hidden
            pack[:, 6 * D + c * D : 6 * D + (c + 1) * D] = saved["activated"][:, cols]
        grad_second = grad_second + dot_nt(grad_hidden, wa[4 + c])
    grad_scale_m = token_sum(grad_second * normed_two)
    grad_shift_m = token_sum(grad_second)
    grad_middle = grad_y + norm_back(grad_second * (1.0 + row(4)), normed_two, inverse_two)
    grad_gate_a = token_sum(grad_middle * attended)
    return grad_middle, (grad_gate_a, grad_shift_m, grad_scale_m, grad_gate_m)


def backward_attention(grad_middle, z, mod, wa, saved, pack=None):
    row = lambda i: mod[i : i + 1, :]
    normed, inverse = normalize(z)
    grad_attended = (row(2) * grad_middle).astype(bf16)
    grad_mixture = dot_nt(grad_attended, wa[3]).astype(bf16)
    low_half = half_masks()
    grads = [[], [], []]
    zero = jnp.zeros((SEQ, PAIR), bf16)
    for pair in range(H // 2):
        cols = [slice(j * D + pair * PAIR, j * D + (pair + 1) * PAIR) for j in range(3)]
        q, k, v = (saved["qkv"][:, c] for c in cols)
        grad_mix = grad_mixture[:, pair * PAIR : (pair + 1) * PAIR]
        outs = []
        for e in range(2):
            mask = low_half if e == 0 else jnp.logical_not(low_half)
            probs = saved["probs"][pair * 2 + e]
            grad_probs = dot_nt(jnp.where(mask, grad_mix, zero), v)
            wide = probs.astype(f32)
            weighted = grad_probs * wide
            grad_scores = (weighted - wide * jnp.sum(weighted, axis=-1, keepdims=True)).astype(bf16)
            outs.append(
                (
                    dot(grad_scores, k) * HD ** (-0.5),
                    dot_tn(grad_scores, q) * HD ** (-0.5),
                    dot_tn(probs, grad_mix),
                )
            )
        for j in range(3):
            grads[j].append(jnp.where(low_half, outs[0][j], outs[1][j]).astype(bf16))
    grads = [jnp.concatenate(g, axis=1) for g in grads]
    grad_first = dot_nt(grads[0], wa[0]) + dot_nt(grads[1], wa[1]) + dot_nt(grads[2], wa[2])
    if pack is not None:
        pack[:, 0:D] = (normed * (1.0 + row(1)) + row(0)).astype(bf16)
        for j in range(3):
            pack[:, D + j * D : 2 * D + j * D] = grads[j]
        pack[:, 4 * D : 5 * D] = saved["mixture"][...]
        pack[:, 5 * D : 6 * D] = grad_attended
    grad_scale_a = token_sum(grad_first * normed)
    grad_shift_a = token_sum(grad_first)
    grad_in = grad_middle + norm_back(grad_first * (1.0 + row(1)), normed, inverse)
    return grad_in, (grad_shift_a, grad_scale_a)


SAVED = (
    ("qkv", (SEQ, 3 * D), bf16),
    ("probs", (H, SEQ, SEQ), bf16),
    ("mixture", (SEQ, D), bf16),
    ("attended", (SEQ, D), f32),
    ("activated", (SEQ, FF), bf16),
    ("slope", (SEQ, FF), bf16),
    ("result", (SEQ, D), f32),
)
NAMES = tuple(name for name, _, _ in SAVED)


def weight_copies(scalars, own, other, layer, wa, wd, sem):
    pieces = len(own)
    rows = D // pieces
    dp = scalars[0]
    mine = scalars[2] == layer

    def make(source, k):
        place = jnp.bitwise_xor(dp, k) if pieces > 1 else 0
        start = pl.multiple_of(place * rows, 16)
        first = pltpu.make_async_copy(
            source[k].at[pl.ds(0, 8)], wa.at[:, pl.ds(start, rows), :], sem.at[0, k]
        )
        second = pltpu.make_async_copy(
            source[k].at[pl.ds(8, 4)], wd.at[pl.ds(place * 4, 4)], sem.at[1, k]
        )
        return first, second

    def start():
        for source, chosen in ((own, mine), (other, jnp.logical_not(mine))):

            @pl.when(chosen)
            def _():
                for k in range(pieces):
                    for copy in make(source, k):
                        copy.start()

    def wait():
        for k in range(pieces):
            for copy in make(own, k):
                copy.wait()

    return start, wait


def down_chunk(wd_ref):
    blocks = wd_ref.shape[0]
    per = blocks // CHUNKS
    rows = wd_ref.shape[1]

    def chunk(c):
        return wd_ref[c * per : (c + 1) * per].reshape(per * rows, D)

    return chunk


def put(chosen, keep, give, value):
    @pl.when(chosen)
    def _():
        keep[...] = value

    @pl.when(jnp.logical_not(chosen))
    def _():
        give[...] = value


def forward_kernel(pieces, scalars, latents, arriving, mods, *refs):
    own, other = refs[:pieces], refs[pieces : 2 * pieces]
    rest = refs[2 * pieces :]
    outs, keep, give = rest[:2], rest[2], rest[3]
    saved = [dict(zip(NAMES, rest[4 + 7 * layer : 11 + 7 * layer])) for layer in range(2)]
    wa, wd, sems = rest[18:]
    handles = [
        weight_copies(scalars, own, other, layer, wa.at[layer], wd.at[layer], sems.at[layer])
        for layer in range(2)
    ]
    for start, _ in handles:
        start()
    alive = jnp.where(scalars[3] > 0, 1.0, 0.0).astype(f32)
    z = jnp.where(scalars[1] == 0, latents[scalars[2]], arriving[...])
    for layer in range(2):
        handles[layer][1]()
        z = forward_layer(
            z.astype(f32),
            mods[layer],
            alive,
            wa.at[layer],
            down_chunk(wd.at[layer]),
            saved[layer],
        ).astype(bf16)
        outs[layer][...] = z
        put(scalars[2] == layer, keep, give, z)


def weight_scratch(pieces, layers):
    rows = D // pieces
    return [
        pltpu.VMEM((layers, 8, D, D), bf16),
        pltpu.VMEM((layers, 4 * pieces, rows, D), bf16),
        pltpu.SemaphoreType.DMA((layers, 2, pieces)),
    ]


vmem = pl.BlockSpec(memory_space=pltpu.VMEM)
smem = pl.BlockSpec(memory_space=pltpu.SMEM)
hbm = pl.BlockSpec(memory_space=pl.ANY)


def run_forward(scalars, latents, arriving, mods, own, other):
    pieces = len(own)
    shapes = [jax.ShapeDtypeStruct((SEQ, D), bf16)] * 4
    shapes += [jax.ShapeDtypeStruct(shape, kind) for _, shape, kind in SAVED] * 2
    out = pl.pallas_call(
        partial(forward_kernel, pieces),
        out_shape=shapes,
        in_specs=[smem, vmem, vmem, vmem] + [hbm] * (2 * pieces),
        out_specs=[vmem] * len(shapes),
        scratch_shapes=weight_scratch(pieces, 2),
        compiler_params=pltpu.CompilerParams(vmem_limit_bytes=VMEM_BYTES),
        name="forward",
    )(scalars, latents, arriving, mods, *own, *other)
    return out[:4], (out[4:11], out[11:18])


PACK_M, PACK_A = 10 * D, 6 * D


def backward_kernel(pieces, full, scalars, cots, lats, grad_in, z_in, act, mods, *refs):
    own, other = refs[:pieces], refs[pieces : 2 * pieces]
    rest = refs[2 * pieces :]
    saved = [dict(zip(NAMES, rest[7 * layer : 7 * layer + 7])) for layer in range(2)]
    rest = rest[14:]
    if full:
        keep_z, give_z, grad_mod, keep_pack, give_pack = rest[:5]
        wa, wd, sems, packs, out_sems = rest[5:]
    else:
        out, wa, wd, sems = rest
    handles = [
        weight_copies(scalars, own, other, layer, wa.at[layer], wd.at[layer], sems.at[layer])
        for layer in range(2)
    ]
    for layer in (1, 0):
        handles[layer][0]()
    alive = jnp.where(scalars[3] > 0, 1.0, 0.0).astype(f32)
    upstream = jnp.where(scalars[1] == 1, cots[scalars[2]], grad_in[...])
    inputs = [jnp.where(scalars[1] == 0, lats[scalars[2]], z_in[...]), act[...]]
    for layer in (1, 0):
        chosen = scalars[2] == layer
        handles[layer][1]()
        if full:
            pack = packs.at[jnp.where(chosen, 0, 1)]
            pack_m, pack_a = pack.at[:, pl.ds(0, PACK_M)], pack.at[:, pl.ds(PACK_M, PACK_A)]
        else:
            pack_m, pack_a = None, None
        z = inputs[layer].astype(f32)
        grad_middle, four = backward_mlp(
            upstream.astype(f32),
            z,
            mods[layer],
            alive,
            wa.at[layer],
            down_chunk(wd.at[layer]),
            saved[layer],
            pack_m,
        )
        grad_z, two = backward_attention(
            grad_middle, z, mods[layer], wa.at[layer], saved[layer], pack_a
        )
        upstream = grad_z.astype(bf16)
        if full:
            put(chosen, keep_z, give_z, upstream)
            grad_mod[layer] = jnp.concatenate(two + four, axis=0)

            for take, slot, target in ((chosen, 0, keep_pack), (jnp.logical_not(chosen), 1, give_pack)):

                @pl.when(take)
                def _():
                    pltpu.make_async_copy(packs.at[slot], target, out_sems.at[slot]).start()
        else:
            if layer == 0:
                out[...] = upstream
    if full:
        for slot, target in enumerate((keep_pack, give_pack)):
            pltpu.make_async_copy(packs.at[slot], target, out_sems.at[slot]).wait()


def run_backward(full, scalars, cots, lats, grad_in, z_in, act, mods, own, other, saved):
    pieces = len(own)
    shapes = [jax.ShapeDtypeStruct((SEQ, D), bf16)]
    specs = [vmem]
    scratch = weight_scratch(pieces, 2)
    if full:
        shapes = shapes * 2 + [jax.ShapeDtypeStruct((2, 6, D), f32)]
        shapes += [jax.ShapeDtypeStruct((SEQ, PACK_M + PACK_A), bf16)] * 2
        specs = [vmem] * 3 + [hbm] * 2
        scratch += [pltpu.VMEM((2, SEQ, PACK_M + PACK_A), bf16), pltpu.SemaphoreType.DMA((2,))]
    return pl.pallas_call(
        partial(backward_kernel, pieces, full),
        out_shape=shapes,
        in_specs=[smem] + [vmem] * 6 + [hbm] * (2 * pieces) + [vmem] * 14,
        out_specs=specs,
        scratch_shapes=scratch,
        compiler_params=pltpu.CompilerParams(vmem_limit_bytes=VMEM_BYTES),
        name="backward",
    )(scalars, cots, lats, grad_in, z_in, act, mods, *own, *other, *saved[0], *saved[1])


def weight_grad_kernel(pieces, scalars, keep, got, *refs):
    outs, (block, tall) = refs[:pieces], refs[pieces:]
    rows = D // pieces
    dp = scalars[0]

    def places(k):
        return jnp.bitwise_xor(dp, k) if pieces > 1 else 0

    def product(a, b):
        left, right = slice(a * D, (a + 1) * D), slice(b * D, (b + 1) * D)
        return (
            dot_tn(keep[:, left], keep[:, right]) + dot_tn(got[:, left], got[:, right])
        ).astype(bf16)

    pairs = [(10, 11), (10, 12), (10, 13), (14, 15)] + [(0, 2 + c) for c in range(4)]
    for j, pair in enumerate(pairs):
        block[j] = product(*pair)
    for c in range(CHUNKS):
        tall[c * D : (c + 1) * D, :] = product(6 + c, 1)
    for k in range(pieces):
        start = pl.multiple_of(places(k) * rows, 16)
        outs[k][0:8] = block[:, pl.ds(start, rows), :]
        start = pl.multiple_of(places(k) * 4 * rows, 16)
        outs[k][8:12] = tall[pl.ds(start, 4 * rows), :].reshape(4, rows, D)


def run_weight_grad(pieces, scalars, keep, got):
    rows = D // pieces
    return pl.pallas_call(
        partial(weight_grad_kernel, pieces),
        out_shape=[jax.ShapeDtypeStruct((BLOCKS, rows, D), bf16)] * pieces,
        in_specs=[smem] + [vmem] * 2,
        out_specs=[vmem] * pieces,
        scratch_shapes=[pltpu.VMEM((8, D, D), bf16), pltpu.VMEM((FF, D), bf16)],
        compiler_params=pltpu.CompilerParams(vmem_limit_bytes=VMEM_BYTES),
        name="weight_grad",
    )(scalars, keep, got)


def swap(value, axis, bit):
    count = lax.axis_size(axis)
    return lax.ppermute(value, axis, [(i, i ^ bit) for i in range(count)])


def one_way(value, axis, source, target):
    return lax.ppermute(value, axis, [(source, target)])


def exchange(value, axes):
    return lax.all_to_all(value, axes, split_axis=0, concat_axis=0, tiled=True)


def spread(value, axes):
    return exchange(jnp.broadcast_to(value[None], (lax.axis_size(axes), *value.shape)), axes)


def local(
    latents_in,
    cotangent,
    labels,
    timesteps,
    counts,
    label_table,
    time_table,
    adaptive_norm_weight,
    adaptive_norm_bias,
    query_key_value_weight,
    attention_output_weight,
    up_weight,
    down_weight,
):
    dp_count = lax.axis_size("dp")
    dp, x, core = (lax.axis_index(name) for name in ("dp", "x", "core"))
    rows = D // dp_count
    small = dp_count == 8
    latents = latents_in[:, 0]
    cotangents = cotangent[:, 0]
    live = jnp.where(core == 0, counts[0, 0], counts[1, 0])
    scalars = jnp.stack([dp, x, core, live]).astype(jnp.int32)

    ids = spread(jnp.concatenate([labels[:, 0], timesteps[:, 0]]), "dp")
    ids = ids.reshape(dp_count, 2, MICRO).transpose(1, 2, 0).reshape(2, MICRO * dp_count)

    blocks = jnp.concatenate(
        [
            query_key_value_weight[0].reshape(rows, 3, D).transpose(1, 0, 2),
            attention_output_weight[0][None],
            up_weight[0].reshape(rows, CHUNKS, D).transpose(1, 0, 2),
        ],
        axis=0,
    )
    if small:
        shard = jnp.concatenate([blocks, down_weight[0].reshape(CHUNKS, rows, D)], axis=0)
        own = {0: shard, 2: swap(shard, "dp", 2), 4: swap(shard, "dp", 4), 1: swap(shard, "dp", 1)}
        shard, ids, own[1], own[2], own[4] = lax.optimization_barrier(
            (shard, ids, own[1], own[2], own[4])
        )
        own[6] = swap(shard, "dp", 6)
        own[3], own[5] = swap(own[2], "dp", 1), swap(own[4], "dp", 1)
    else:
        own = [
            jnp.concatenate(
                [
                    lax.all_gather(blocks, "dp", axis=1, tiled=True),
                    lax.all_gather(down_weight[0], "dp", axis=0, tiled=True).reshape(CHUNKS, D, D),
                ],
                axis=0,
            )
        ]

    condition = label_table[ids[0]] + time_table[ids[1]]
    condition = lax.dynamic_slice_in_dim(condition, dp * rows, rows, axis=1)
    cond_act = jax.nn.silu(condition).astype(bf16)
    ada = adaptive_norm_weight[0]
    width = 6 * D // dp_count
    bias = lax.dynamic_update_slice_in_dim(
        jnp.zeros((6 * D,), f32), adaptive_norm_bias[0].astype(f32), dp * width, 0
    )
    linear = jnp.dot(cond_act, ada, preferred_element_type=f32) + bias
    linear = exchange(linear, ("core", "dp"))
    mods = jnp.sum(linear.reshape(2, dp_count, 6 * D), axis=1).reshape(2, 6, D)
    if small:
        own[6], mods, own[3], own[5] = lax.optimization_barrier((own[6], mods, own[3], own[5]))
        own[7] = swap(own[6], "dp", 1)
        own = [own[k] for k in range(8)]
    pieces = len(own)
    other = [swap(piece, "core", 1) for piece in own]

    arriving = jnp.zeros((SEQ, D), bf16)
    (_, leaving, _, _), _ = run_forward(scalars, latents, arriving, mods, own, other)
    arriving = one_way(leaving, "x", 0, 1)
    (act_a, _, keep_act, give_act), saved = run_forward(
        scalars, latents, arriving, mods, own, other
    )

    def both_micros(mine, theirs):
        return jnp.where(core == 0, jnp.stack([mine, theirs]), jnp.stack([theirs, mine]))

    operands = (arriving, act_a, mods, own, other, saved)
    grad_in = jnp.zeros((SEQ, D), bf16)
    (grad_out,) = run_backward(False, scalars, cotangents, latents, grad_in, *operands)
    grad_in = one_way(grad_out, "x", 1, 0)
    keep_z, give_z, grad_mod, keep_pack, give_pack = run_backward(
        True, scalars, cotangents, latents, grad_in, *operands
    )
    got_pack = swap(give_pack, "core", 1)
    parts = list(run_weight_grad(pieces, scalars, keep_pack, got_pack))
    if small:
        across = {k: swap(parts[2 * k + 1], "dp", 1) for k in (3, 2, 1, 0)}
        sums = {k: parts[2 * k].astype(f32) + across[k].astype(f32) for k in (3, 2, 1, 0)}
        far = [swap(sums[k].astype(bf16), "dp", 2 * k) for k in (3, 2, 1)]
        total = sums[0]
        for piece in far:
            total = total + piece.astype(f32)
    else:
        square = lax.psum_scatter(
            parts[0][:8].astype(f32), "dp", scatter_dimension=1, tiled=True
        )
        tall = lax.psum_scatter(
            parts[0][8:].astype(f32).reshape(FF, D), "dp", scatter_dimension=0, tiled=True
        )
        total = jnp.concatenate([square, tall.reshape(CHUNKS, rows, D)], axis=0)
    acts = both_micros(keep_act, swap(give_act, "core", 1))
    act_grads = both_micros(keep_z, swap(give_z, "core", 1))

    grad_mod = jnp.broadcast_to(grad_mod.reshape(2, 1, 6 * D), (2, dp_count, 6 * D))
    grad_mod = exchange(grad_mod.reshape(2 * dp_count, 6 * D), ("core", "dp"))
    grad_mod_low = grad_mod.astype(bf16)
    grad_w_ada = jnp.dot(cond_act.T, grad_mod_low, preferred_element_type=f32)
    grad_b_ada = lax.dynamic_slice_in_dim(jnp.sum(grad_mod, axis=0), dp * width, width)
    _, silu_pull = jax.vjp(jax.nn.silu, condition)
    grad_cond = silu_pull(
        lax.dot_general(grad_mod_low, ada, (((1,), (1,)), ((), ())), preferred_element_type=f32)
    )[0]
    table_rows = spread(grad_cond, ("x", "core", "dp"))
    table_rows = jnp.sum(table_rows.reshape(4, dp_count, MICRO * dp_count, rows), axis=0)
    table_rows = table_rows.transpose(1, 0, 2).reshape(MICRO * dp_count, D)
    share = CLASSES // (4 * dp_count)
    base = ((x * 2 + core) * dp_count + dp) * share
    targets = base + jnp.arange(share, dtype=jnp.int32)
    label_hot = (targets[:, None] == ids[0][None, :]).astype(f32)
    time_hot = (targets[:, None] == ids[1][None, :]).astype(f32)
    label_part = jnp.dot(label_hot, table_rows, precision=highest)
    time_part = jnp.dot(time_hot, table_rows, precision=highest)

    grad_w_qkv = total[0:3].transpose(1, 0, 2).reshape(rows, 3 * D)
    grad_w_out = total[3]
    grad_w_up = total[4:8].transpose(1, 0, 2).reshape(rows, FF)
    grad_w_down = total[8:12].reshape(CHUNKS * rows, D)

    return (
        acts[None, :, None],
        act_grads[None, :, None],
        grad_w_ada[None],
        grad_b_ada[None],
        grad_w_qkv[None],
        grad_w_out[None],
        grad_w_up[None],
        grad_w_down[None],
        label_part,
        time_part,
    )


def solution(mesh):
    sections, dp_count = mesh.devices.shape
    grid = Mesh(mesh.devices.reshape(2, sections // 2, dp_count), ("x", "core", "dp"))
    section = ("x", "core")
    return jax.shard_map(
        local,
        mesh=grid,
        in_specs=(
            P(None, "dp", None, None),
            P(None, "dp", None, None),
            P(None, "dp"),
            P(None, "dp"),
            P(None, "dp"),
            P(),
            P(),
            P(section, "dp", None),
            P(section, "dp"),
            P(section, "dp", None),
            P(section, "dp", None),
            P(section, "dp", None),
            P(section, "dp", None),
        ),
        out_specs=(
            P(section, None, "dp", None, None),
            P(section, None, "dp", None, None),
            P(section, "dp", None),
            P(section, "dp"),
            P(section, "dp", None),
            P(section, "dp", None),
            P(section, "dp", None),
            P(section, "dp", None),
            P(("x", "core", "dp"), None),
            P(("x", "core", "dp"), None),
        ),
        check_vma=False,
    )
```

```python
from functools import partial

import jax
import jax.numpy as jnp
from jax import lax
from jax.experimental import pallas as pl
from jax.experimental.pallas import tpu as pltpu
from jax.sharding import Mesh, PartitionSpec as P

D = 384
H = 6
HD = 64
FF = 1536
SEQ = 256
CLASSES = 1024
MICRO = 2
BLOCKS = 12
CHUNKS = FF // D
PAIR = 2 * HD

epsilon = 1e-06
highest = lax.Precision.HIGHEST
f32 = jnp.float32
bf16 = jnp.bfloat16


def dot(a, b):
    return lax.dot_general(a, b, (((1,), (0,)), ((), ())), preferred_element_type=f32)


def dot_nt(a, b):
    return lax.dot_general(a, b, (((1,), (1,)), ((), ())), preferred_element_type=f32)


def dot_tn(a, b):
    return lax.dot_general(a, b, (((0,), (0,)), ((), ())), preferred_element_type=f32)


def normalize(values):
    center = values - jnp.mean(values, axis=-1, keepdims=True)
    inverse = lax.rsqrt(jnp.mean(center * center, axis=-1, keepdims=True) + epsilon)
    return center * inverse, inverse


def norm_back(upstream, normed, inverse):
    return inverse * (
        upstream
        - jnp.mean(upstream, axis=-1, keepdims=True)
        - normed * jnp.mean(upstream * normed, axis=-1, keepdims=True)
    )


def token_sum(values):
    return jnp.sum(values, axis=0, keepdims=True)


def half_masks():
    lane = lax.broadcasted_iota(jnp.int32, (SEQ, PAIR), 1)
    return lane < HD


def forward_layer(z, mod, alive, wa, wd, saved):
    def save(name, where, value):
        if saved is not None:
            saved[name][where] = value

    row = lambda i: mod[i : i + 1, :]
    normed, _ = normalize(z)
    first_in = (normed * (1.0 + row(1)) + row(0)).astype(bf16)
    parts = [dot(first_in, wa[j]).astype(bf16) for j in range(3)]
    for j in range(3):
        save("qkv", (slice(None), slice(j * D, (j + 1) * D)), parts[j])
    low_half = half_masks()
    mixed = []
    for pair in range(H // 2):
        cols = slice(pair * PAIR, (pair + 1) * PAIR)
        q, k, v = (part[:, cols] for part in parts)
        outs = []
        for e in range(2):
            mask = low_half if e == 0 else jnp.logical_not(low_half)
            q_e = jnp.where(mask, q * HD ** (-0.5), 0).astype(bf16)
            scores = dot_nt(q_e, k)
            grown = jnp.exp(scores - jnp.max(scores, axis=-1, keepdims=True))
            probs = (grown * (1.0 / jnp.sum(grown, axis=-1, keepdims=True))).astype(bf16)
            save("probs", pair * 2 + e, probs)
            outs.append(dot(probs, v))
        mixed.append(jnp.where(low_half, outs[0], outs[1]).astype(bf16))
    mixture = jnp.concatenate(mixed, axis=1)
    save("mixture", ..., mixture)
    attended = dot(mixture, wa[3])
    save("attended", ..., attended)
    middle = z + row(2) * attended
    normed_two, _ = normalize(middle)
    second_in = (normed_two * (1.0 + row(4)) + row(3)).astype(bf16)
    result = jnp.zeros((SEQ, D), f32)
    c0 = (2.0 / jnp.pi) ** 0.5
    for c in range(CHUNKS):
        cols = slice(c * D, (c + 1) * D)
        hidden = dot(second_in, wa[4 + c])
        square = hidden * hidden
        tanh = jnp.tanh(c0 * hidden * (1.0 + 0.044715 * square))
        half = 0.5 * (1.0 + tanh)
        activated = (hidden * half).astype(bf16)
        save("activated", (slice(None), cols), activated)
        if saved is not None:
            bend = 0.5 * hidden * (1.0 - tanh * tanh)
            slope = half + bend * (c0 * (1.0 + 3 * 0.044715 * square))
            save("slope", (slice(None), cols), slope.astype(bf16))
        result = result + dot(activated, wd(c))
    save("result", ..., result)
    return (middle + row(5) * result) * alive


def backward_mlp(grad_out, z, mod, alive, wa, wd, saved, pack=None):
    row = lambda i: mod[i : i + 1, :]
    attended = saved["attended"][...]
    middle = z + row(2) * attended
    normed_two, inverse_two = normalize(middle)
    grad_y = grad_out * alive
    grad_gate_m = token_sum(grad_y * saved["result"][...])
    grad_result = (row(5) * grad_y).astype(bf16)
    grad_second = jnp.zeros((SEQ, D), f32)
    if pack is not None:
        pack[:, 0:D] = (normed_two * (1.0 + row(4)) + row(3)).astype(bf16)
        pack[:, D : 2 * D] = grad_result
    for c in range(CHUNKS):
        cols = slice(c * D, (c + 1) * D)
        grad_act = dot_nt(grad_result, wd(c))
        grad_hidden = (grad_act * saved["slope"][:, cols].astype(f32)).astype(bf16)
        if pack is not None:
            pack[:, 2 * D + c * D : 2 * D + (c + 1) * D] = grad_hidden
        grad_second = grad_second + dot_nt(grad_hidden, wa[4 + c])
    grad_scale_m = token_sum(grad_second * normed_two)
    grad_shift_m = token_sum(grad_second)
    grad_middle = grad_y + norm_back(grad_second * (1.0 + row(4)), normed_two, inverse_two)
    grad_gate_a = token_sum(grad_middle * attended)
    return grad_middle, (grad_gate_a, grad_shift_m, grad_scale_m, grad_gate_m)


def backward_attention(grad_middle, z, mod, wa, saved, pack=None):
    row = lambda i: mod[i : i + 1, :]
    normed, inverse = normalize(z)
    grad_attended = (row(2) * grad_middle).astype(bf16)
    grad_mixture = dot_nt(grad_attended, wa[3]).astype(bf16)
    low_half = half_masks()
    grads = [[], [], []]
    zero = jnp.zeros((SEQ, PAIR), bf16)
    for pair in range(H // 2):
        cols = [slice(j * D + pair * PAIR, j * D + (pair + 1) * PAIR) for j in range(3)]
        q, k, v = (saved["qkv"][:, c] for c in cols)
        grad_mix = grad_mixture[:, pair * PAIR : (pair + 1) * PAIR]
        outs = []
        for e in range(2):
            mask = low_half if e == 0 else jnp.logical_not(low_half)
            probs = saved["probs"][pair * 2 + e]
            grad_probs = dot_nt(jnp.where(mask, grad_mix, zero), v)
            wide = probs.astype(f32)
            weighted = grad_probs * wide
            grad_scores = (weighted - wide * jnp.sum(weighted, axis=-1, keepdims=True)).astype(bf16)
            outs.append(
                (
                    dot(grad_scores, k) * HD ** (-0.5),
                    dot_tn(grad_scores, q) * HD ** (-0.5),
                    dot_tn(probs, grad_mix),
                )
            )
        for j in range(3):
            grads[j].append(jnp.where(low_half, outs[0][j], outs[1][j]).astype(bf16))
    grads = [jnp.concatenate(g, axis=1) for g in grads]
    grad_first = dot_nt(grads[0], wa[0]) + dot_nt(grads[1], wa[1]) + dot_nt(grads[2], wa[2])
    if pack is not None:
        pack[:, 0:D] = (normed * (1.0 + row(1)) + row(0)).astype(bf16)
        for j in range(3):
            pack[:, D + j * D : 2 * D + j * D] = grads[j]
        pack[:, 5 * D : 6 * D] = grad_attended
    grad_scale_a = token_sum(grad_first * normed)
    grad_shift_a = token_sum(grad_first)
    grad_in = grad_middle + norm_back(grad_first * (1.0 + row(1)), normed, inverse)
    return grad_in, (grad_shift_a, grad_scale_a)


SAVED = (
    ("qkv", (SEQ, 3 * D), bf16),
    ("probs", (H, SEQ, SEQ), bf16),
    ("mixture", (SEQ, D), bf16),
    ("attended", (SEQ, D), f32),
    ("activated", (SEQ, FF), bf16),
    ("slope", (SEQ, FF), bf16),
    ("result", (SEQ, D), f32),
)
NAMES = tuple(name for name, _, _ in SAVED)


def weight_copies(scalars, own, other, layer, wa, wd, sem):
    pieces = len(own)
    rows = D // pieces
    dp = scalars[0]
    mine = scalars[2] == layer

    def make(source, k):
        place = jnp.bitwise_xor(dp, k) if pieces > 1 else 0
        start = pl.multiple_of(place * rows, 16)
        first = pltpu.make_async_copy(
            source[k].at[pl.ds(0, 8)], wa.at[:, pl.ds(start, rows), :], sem.at[0, k]
        )
        second = pltpu.make_async_copy(
            source[k].at[pl.ds(8, 4)], wd.at[pl.ds(place * 4, 4)], sem.at[1, k]
        )
        return first, second

    def start():
        for source, chosen in ((own, mine), (other, jnp.logical_not(mine))):

            @pl.when(chosen)
            def _():
                for k in range(pieces):
                    for copy in make(source, k):
                        copy.start()

    def wait():
        for k in range(pieces):
            for copy in make(own, k):
                copy.wait()

    return start, wait


def down_chunk(wd_ref):
    blocks = wd_ref.shape[0]
    per = blocks // CHUNKS
    rows = wd_ref.shape[1]

    def chunk(c):
        return wd_ref[c * per : (c + 1) * per].reshape(per * rows, D)

    return chunk


def put(chosen, keep, give, value):
    @pl.when(chosen)
    def _():
        keep[...] = value

    @pl.when(jnp.logical_not(chosen))
    def _():
        give[...] = value


def weight_scratch(pieces, layers):
    rows = D // pieces
    return [
        pltpu.VMEM((layers, 8, D, D), bf16),
        pltpu.VMEM((layers, 4 * pieces, rows, D), bf16),
        pltpu.SemaphoreType.DMA((layers, 2, pieces)),
    ]


vmem = pl.BlockSpec(memory_space=pltpu.VMEM)
smem = pl.BlockSpec(memory_space=pltpu.SMEM)
hbm = pl.BlockSpec(memory_space=pl.ANY)
sent = pl.BlockSpec(memory_space=pltpu.HBM)


PACK_M, PACK_A = 10 * D, 6 * D
packs_shape = (SEQ, PACK_M + PACK_A)


def layer_weights(scalars, own, other, wa, wd, sems, order):
    handles = [
        weight_copies(scalars, own, other, layer, wa.at[layer], wd.at[layer], sems.at[layer])
        for layer in range(2)
    ]
    for layer in order:
        handles[layer][0]()
    return [handle[1] for handle in handles]


def live_factor(scalars):
    return jnp.where(scalars[3] > 0, 1.0, 0.0).astype(f32)


def first_kernel(pieces, scalars, latents, mods, *refs):
    own, other = refs[:pieces], refs[pieces : 2 * pieces]
    out, wa, wd, sems = refs[2 * pieces :]
    waits = layer_weights(scalars, own, other, wa, wd, sems, (0, 1))
    z = latents[scalars[2]]
    for layer in range(2):
        waits[layer]()
        weights = wa.at[layer], down_chunk(wd.at[layer])
        z = forward_layer(z.astype(f32), mods[layer], live_factor(scalars), *weights, None)
        z = z.astype(bf16)
    out[...] = z


def middle_kernel(pieces, scalars, latents, arriving, cots, mods, *refs):
    own, other = refs[:pieces], refs[pieces : 2 * pieces]
    rest = refs[2 * pieces :]
    act_a, keep, give, out = rest[:4]
    kept, (wa, wd, sems) = rest[4:18], rest[18:]
    saved = [dict(zip(NAMES, kept[7 * layer : 7 * layer + 7])) for layer in range(2)]
    waits = layer_weights(scalars, own, other, wa, wd, sems, (0, 1))
    weights = [(wa.at[layer], down_chunk(wd.at[layer])) for layer in range(2)]
    alive = live_factor(scalars)
    z = jnp.where(scalars[1] == 0, latents[scalars[2]], arriving[...])
    inputs = []
    for layer in range(2):
        waits[layer]()
        inputs.append(z)
        z = forward_layer(z.astype(f32), mods[layer], alive, *weights[layer], saved[layer])
        z = z.astype(bf16)
        put(scalars[2] == layer, keep, give, z)
        if layer == 0:
            act_a[...] = z
    upstream = cots[scalars[2]]
    for layer in (1, 0):
        z = inputs[layer] if layer == 0 else act_a[...]
        z = z.astype(f32)
        grad_middle, _ = backward_mlp(
            upstream.astype(f32), z, mods[layer], alive, *weights[layer], saved[layer]
        )
        grad_z, _ = backward_attention(grad_middle, z, mods[layer], wa.at[layer], saved[layer])
        upstream = grad_z.astype(bf16)
    out[...] = upstream


def last_kernel(pieces, scalars, cots, lats, grad_in, z_in, act, mods, *refs):
    own, other = refs[:pieces], refs[pieces : 2 * pieces]
    rest = refs[2 * pieces :]
    kept, rest = rest[:14], rest[14:]
    keep_z, give_z, grad_mod, keep_pack, give_pack = rest[:5]
    wa, wd, sems, packs, copy_sems, out_sems = rest[5:]
    saved = [dict(zip(NAMES, kept[7 * layer : 7 * layer + 7])) for layer in range(2)]
    pack = [packs.at[jnp.where(scalars[2] == layer, 0, 1)] for layer in range(2)]
    direct = (("activated", pl.ds(6 * D, FF)), ("mixture", pl.ds(PACK_M + 4 * D, D)))
    copies = [
        pltpu.make_async_copy(saved[layer][name], pack[layer].at[:, cols], copy_sems.at[layer, i])
        for layer in range(2)
        for i, (name, cols) in enumerate(direct)
    ]
    waits = layer_weights(scalars, own, other, wa, wd, sems, (1, 0))
    for copy in copies:
        copy.start()
    alive = live_factor(scalars)
    upstream = jnp.where(scalars[1] == 1, cots[scalars[2]], grad_in[...])
    for layer in (1, 0):
        chosen = scalars[2] == layer
        waits[layer]()
        pack_m = pack[layer].at[:, pl.ds(0, PACK_M)]
        pack_a = pack[layer].at[:, pl.ds(PACK_M, PACK_A)]
        z = act[...] if layer == 1 else jnp.where(scalars[1] == 0, lats[scalars[2]], z_in[...])
        z = z.astype(f32)
        grad_middle, four = backward_mlp(
            upstream.astype(f32),
            z,
            mods[layer],
            alive,
            wa.at[layer],
            down_chunk(wd.at[layer]),
            saved[layer],
            pack_m,
        )
        grad_z, two = backward_attention(
            grad_middle, z, mods[layer], wa.at[layer], saved[layer], pack_a
        )
        upstream = grad_z.astype(bf16)
        put(chosen, keep_z, give_z, upstream)
        grad_mod[layer] = jnp.concatenate(two + four, axis=0)
        for copy in copies[2 * layer : 2 * layer + 2]:
            copy.wait()
        for take, slot, target in (
            (chosen, 0, keep_pack),
            (jnp.logical_not(chosen), 1, give_pack),
        ):

            @pl.when(take)
            def _():
                pltpu.make_async_copy(packs.at[slot], target, out_sems.at[slot]).start()

    for slot, target in enumerate((keep_pack, give_pack)):
        pltpu.make_async_copy(packs.at[slot], target, out_sems.at[slot]).wait()


token_shape = jax.ShapeDtypeStruct((SEQ, D), bf16)
saved_shapes = [jax.ShapeDtypeStruct(shape, kind) for _, shape, kind in SAVED] * 2


def limit(mebibytes):
    return pltpu.CompilerParams(vmem_limit_bytes=mebibytes * 1024 * 1024)


def run_first(scalars, latents, mods, own, other):
    pieces = len(own)
    return pl.pallas_call(
        partial(first_kernel, pieces),
        out_shape=token_shape,
        in_specs=[smem, vmem, vmem] + [hbm] * (2 * pieces),
        out_specs=vmem,
        scratch_shapes=weight_scratch(pieces, 2),
        compiler_params=limit(12),
        name="first",
    )(scalars, latents, mods, *own, *other)


def run_middle(scalars, latents, arriving, cots, mods, own, other):
    pieces = len(own)
    out = pl.pallas_call(
        partial(middle_kernel, pieces),
        out_shape=[token_shape] * 4 + saved_shapes,
        in_specs=[smem] + [vmem] * 4 + [hbm] * (2 * pieces),
        out_specs=[vmem] * 18,
        scratch_shapes=weight_scratch(pieces, 2),
        compiler_params=limit(14),
        name="middle",
    )(scalars, latents, arriving, cots, mods, *own, *other)
    return out[:4], out[4:]


def run_last(scalars, cots, lats, grad_in, z_in, act, mods, own, other, saved):
    pieces = len(own)
    pack = jax.ShapeDtypeStruct(packs_shape, bf16)
    return pl.pallas_call(
        partial(last_kernel, pieces),
        out_shape=[token_shape] * 2 + [jax.ShapeDtypeStruct((2, 6, D), f32)] + [pack] * 2,
        in_specs=[smem] + [vmem] * 6 + [hbm] * (2 * pieces) + [vmem] * 14,
        out_specs=[vmem] * 3 + [sent] * 2,
        scratch_shapes=weight_scratch(pieces, 2)
        + [
            pltpu.VMEM((2, *packs_shape), bf16),
            pltpu.SemaphoreType.DMA((2, 2)),
            pltpu.SemaphoreType.DMA((2,)),
        ],
        compiler_params=limit(20),
        name="last",
    )(scalars, cots, lats, grad_in, z_in, act, mods, *own, *other, *saved)


def weight_grad_kernel(pieces, scalars, keep, got, *refs):
    outs, (packs, block, tall, sems, load_sems) = refs[:pieces], refs[pieces:]
    rows = D // pieces
    dp = scalars[0]
    spans = (pl.ds(PACK_M, PACK_A), pl.ds(0, 6 * D), pl.ds(6 * D, FF))
    loads = [
        [
            pltpu.make_async_copy(source.at[:, span], packs.at[i, :, span], load_sems.at[i, j])
            for i, source in enumerate((keep, got))
        ]
        for j, span in enumerate(spans)
    ]
    for pair in loads:
        for copy in pair:
            copy.start()

    def arrived(j):
        for copy in loads[j]:
            copy.wait()

    def send(stage, k):
        place = jnp.bitwise_xor(dp, k) if pieces > 1 else 0
        if stage == 0:
            start = pl.multiple_of(place * rows, 16)
            source, target = block.at[:, pl.ds(start, rows), :], outs[k].at[pl.ds(0, 8)]
        else:
            source, target = tall.at[pl.ds(place * 4, 4)], outs[k].at[pl.ds(8, 4)]
        return pltpu.make_async_copy(source, target, sems.at[stage, k])

    def product(a, b, wide):
        left, right = slice(a * D, (a + 1) * D), slice(b * D, (b + wide) * D)
        return dot_tn(
            packs[:, :, left].reshape(2 * SEQ, (left.stop - left.start)),
            packs[:, :, right].reshape(2 * SEQ, (right.stop - right.start)),
        ).astype(bf16)

    arrived(0)
    for base, a, b, wide in ((0, 10, 11, 3), (3, 14, 15, 1), (4, 0, 2, 2), (6, 0, 4, 2)):
        if base == 4:
            arrived(1)
        result = product(a, b, wide)
        for j in range(wide):
            block[base + j] = result[:, j * D : (j + 1) * D]
    for k in range(pieces):
        send(0, k).start()
    per = D // rows
    arrived(2)
    for c in range(CHUNKS):
        tall[c * per : (c + 1) * per] = product(6 + c, 1, 1).reshape(per, rows, D)
    for k in range(pieces):
        send(1, k).start()
    for k in range(pieces):
        send(0, k).wait()
        send(1, k).wait()


def run_weight_grad(pieces, scalars, keep, got):
    rows = D // pieces
    return pl.pallas_call(
        partial(weight_grad_kernel, pieces),
        out_shape=[jax.ShapeDtypeStruct((BLOCKS, rows, D), bf16)] * pieces,
        in_specs=[smem] + [hbm] * 2,
        out_specs=[sent] * pieces,
        scratch_shapes=[
            pltpu.VMEM((2, *packs_shape), bf16),
            pltpu.VMEM((8, D, D), bf16),
            pltpu.VMEM((FF // rows, rows, D), bf16),
            pltpu.SemaphoreType.DMA((2, pieces)),
            pltpu.SemaphoreType.DMA((2, 3)),
        ],
        compiler_params=limit(58),
        name="weight_grad",
    )(scalars, keep, got)


def total_kernel(*refs):
    parts, (qkv, out, up, down) = refs[:5], refs[5:]
    rows = out.shape[0]

    def total(j):
        value = parts[0][j].astype(f32)
        for part in parts[1:]:
            value = value + part[j].astype(f32)
        return value

    for j in range(3):
        qkv[:, j * D : (j + 1) * D] = total(j)
    out[...] = total(3)
    for c in range(CHUNKS):
        up[:, c * D : (c + 1) * D] = total(4 + c)
        down[c * rows : (c + 1) * rows, :] = total(8 + c)


def run_total(*parts):
    rows = parts[0].shape[1]
    shapes = ((rows, 3 * D), (rows, D), (rows, FF), (CHUNKS * rows, D))
    return pl.pallas_call(
        total_kernel,
        out_shape=[jax.ShapeDtypeStruct(shape, f32) for shape in shapes],
        in_specs=[vmem] * 5,
        out_specs=[vmem] * 4,
        compiler_params=limit(4),
        name="total",
    )(*parts)


def joined(first, second):
    return (first.astype(f32) + second.astype(f32)).astype(bf16)


def swap(value, axis, bit):
    count = lax.axis_size(axis)
    return lax.ppermute(value, axis, [(i, i ^ bit) for i in range(count)])


def one_way(value, axis, source, target):
    return lax.ppermute(value, axis, [(source, target)])


def exchange(value, axes):
    return lax.all_to_all(value, axes, split_axis=0, concat_axis=0, tiled=True)


def spread(value, axes):
    return exchange(jnp.broadcast_to(value[None], (lax.axis_size(axes), *value.shape)), axes)


def local(
    latents_in,
    cotangent,
    labels,
    timesteps,
    counts,
    label_table,
    time_table,
    adaptive_norm_weight,
    adaptive_norm_bias,
    query_key_value_weight,
    attention_output_weight,
    up_weight,
    down_weight,
):
    dp_count = lax.axis_size("dp")
    dp, x, core = (lax.axis_index(name) for name in ("dp", "x", "core"))
    rows = D // dp_count
    small = dp_count == 8
    latents = latents_in[:, 0]
    cotangents = cotangent[:, 0]
    live = jnp.where(core == 0, counts[0, 0], counts[1, 0])
    scalars = jnp.stack([dp, x, core, live]).astype(jnp.int32)

    ids = spread(jnp.concatenate([labels[:, 0], timesteps[:, 0]]), "dp")
    ids = ids.reshape(dp_count, 2, MICRO).transpose(1, 2, 0).reshape(2, MICRO * dp_count)

    if small:
        shard = jnp.concatenate(
            [
                query_key_value_weight[0].reshape(rows, 3, D).transpose(1, 0, 2),
                attention_output_weight[0][None],
                up_weight[0].reshape(rows, CHUNKS, D).transpose(1, 0, 2),
                down_weight[0].reshape(CHUNKS, rows, D),
            ],
            axis=0,
        )
        own = {0: shard, 2: swap(shard, "dp", 2), 4: swap(shard, "dp", 4), 1: swap(shard, "dp", 1)}
        shard, ids, own[1], own[2], own[4] = lax.optimization_barrier(
            (shard, ids, own[1], own[2], own[4])
        )
        own[6] = swap(shard, "dp", 6)
        own[3], own[5] = swap(own[2], "dp", 1), swap(own[4], "dp", 1)
    else:
        blocks = jnp.concatenate(
            [
                query_key_value_weight[0].reshape(rows, 3, D).transpose(1, 0, 2),
                attention_output_weight[0][None],
                up_weight[0].reshape(rows, CHUNKS, D).transpose(1, 0, 2),
            ],
            axis=0,
        )
        own = [
            jnp.concatenate(
                [
                    lax.all_gather(blocks, "dp", axis=1, tiled=True),
                    lax.all_gather(down_weight[0], "dp", axis=0, tiled=True).reshape(CHUNKS, D, D),
                ],
                axis=0,
            )
        ]

    condition = label_table[ids[0]] + time_table[ids[1]]
    condition = lax.dynamic_slice_in_dim(condition, dp * rows, rows, axis=1)
    cond_act = jax.nn.silu(condition).astype(bf16)
    ada = adaptive_norm_weight[0]
    width = 6 * D // dp_count
    bias = lax.dynamic_update_slice_in_dim(
        jnp.zeros((6 * D,), f32), adaptive_norm_bias[0].astype(f32), dp * width, 0
    )
    linear = jnp.dot(cond_act, ada, preferred_element_type=f32) + bias
    linear = exchange(linear, ("core", "dp"))
    mods = jnp.sum(linear.reshape(2, dp_count, 6 * D), axis=1).reshape(2, 6, D)
    if small:
        own[6], mods, own[3], own[5] = lax.optimization_barrier((own[6], mods, own[3], own[5]))
        own[7] = swap(own[6], "dp", 1)
        own = [own[k] for k in range(8)]
    pieces = len(own)
    other = [swap(piece, "core", 1) for piece in own]

    leaving = run_first(scalars, latents, mods, own, other)
    arriving = one_way(leaving, "x", 0, 1)
    (act_a, keep_act, give_act, grad_out), saved = run_middle(
        scalars, latents, arriving, cotangents, mods, own, other
    )
    grad_in = one_way(grad_out, "x", 1, 0)
    keep_z, give_z, grad_mod, keep_pack, give_pack = run_last(
        scalars, cotangents, latents, grad_in, arriving, act_a, mods, own, other, saved
    )

    def both_micros(mine, theirs):
        return jnp.where(core == 0, jnp.stack([mine, theirs]), jnp.stack([theirs, mine]))

    got_pack = swap(give_pack, "core", 1)
    grad_mod = jnp.broadcast_to(grad_mod.reshape(2, 1, 6 * D), (2, dp_count, 6 * D))
    grad_mod = exchange(grad_mod.reshape(2 * dp_count, 6 * D), ("core", "dp"))
    parts = list(run_weight_grad(pieces, scalars, keep_pack, got_pack))
    across = {}
    if small:
        across = {k: swap(parts[2 * k + 1], "dp", 1) for k in (3, 2, 1, 0)}
        grad_mod, across[3] = lax.optimization_barrier((grad_mod, across[3]))
    grad_mod_low = grad_mod.astype(bf16)
    _, silu_pull = jax.vjp(jax.nn.silu, condition)
    grad_cond = silu_pull(
        lax.dot_general(grad_mod_low, ada, (((1,), (1,)), ((), ())), preferred_element_type=f32)
    )[0]
    if small:
        grad_cond, across[2] = lax.optimization_barrier((grad_cond, across[2]))
        far = [swap(joined(parts[2 * k], across[k]), "dp", 2 * k) for k in (3, 2, 1)]
        weight_grads = run_total(parts[0], across[0], *far)
    else:
        square = lax.psum_scatter(
            parts[0][:8].astype(f32), "dp", scatter_dimension=1, tiled=True
        )
        tall = lax.psum_scatter(
            parts[0][8:].astype(f32).reshape(FF, D), "dp", scatter_dimension=0, tiled=True
        )
        weight_grads = (
            square[0:3].transpose(1, 0, 2).reshape(rows, 3 * D),
            square[3],
            square[4:8].transpose(1, 0, 2).reshape(rows, FF),
            tall,
        )
    acts = both_micros(keep_act, swap(give_act, "core", 1))
    act_grads = both_micros(keep_z, swap(give_z, "core", 1))

    grad_w_ada = jnp.dot(cond_act.T, grad_mod_low, preferred_element_type=f32)
    grad_b_ada = lax.dynamic_slice_in_dim(jnp.sum(grad_mod, axis=0), dp * width, width)
    table_rows = spread(grad_cond, ("x", "core", "dp"))
    table_rows = jnp.sum(table_rows.reshape(4, dp_count, MICRO * dp_count, rows), axis=0)
    table_rows = table_rows.transpose(1, 0, 2).reshape(MICRO * dp_count, D)
    share = CLASSES // (4 * dp_count)
    base = ((x * 2 + core) * dp_count + dp) * share
    targets = base + jnp.arange(share, dtype=jnp.int32)
    label_hot = (targets[:, None] == ids[0][None, :]).astype(f32)
    time_hot = (targets[:, None] == ids[1][None, :]).astype(f32)
    label_part = jnp.dot(label_hot, table_rows, precision=highest)
    time_part = jnp.dot(time_hot, table_rows, precision=highest)

    grad_w_qkv, grad_w_out, grad_w_up, grad_w_down = weight_grads

    return (
        acts[None, :, None],
        act_grads[None, :, None],
        grad_w_ada[None],
        grad_b_ada[None],
        grad_w_qkv[None],
        grad_w_out[None],
        grad_w_up[None],
        grad_w_down[None],
        label_part,
        time_part,
    )


def solution(mesh):
    sections, dp_count = mesh.devices.shape
    grid = Mesh(mesh.devices.reshape(2, sections // 2, dp_count), ("x", "core", "dp"))
    section = ("x", "core")
    return jax.shard_map(
        local,
        mesh=grid,
        in_specs=(
            P(None, "dp", None, None),
            P(None, "dp", None, None),
            P(None, "dp"),
            P(None, "dp"),
            P(None, "dp"),
            P(),
            P(),
            P(section, "dp", None),
            P(section, "dp"),
            P(section, "dp", None),
            P(section, "dp", None),
            P(section, "dp", None),
            P(section, "dp", None),
        ),
        out_specs=(
            P(section, None, "dp", None, None),
            P(section, None, "dp", None, None),
            P(section, "dp", None),
            P(section, "dp"),
            P(section, "dp", None),
            P(section, "dp", None),
            P(section, "dp", None),
            P(section, "dp", None),
            P(("x", "core", "dp"), None),
            P(("x", "core", "dp"), None),
        ),
        check_vma=False,
    )
```

```python
from functools import partial

import jax
import jax.numpy as jnp
from jax import lax
from jax.experimental import pallas as pl
from jax.experimental.pallas import tpu as pltpu
from jax.sharding import Mesh, PartitionSpec as P

D = 384
H = 6
HD = 64
FF = 1536
SEQ = 256
CLASSES = 1024
MICRO = 2
BLOCKS = 12
CHUNKS = FF // D
PAIR = 2 * HD

epsilon = 1e-06
highest = lax.Precision.HIGHEST
f32 = jnp.float32
bf16 = jnp.bfloat16


def dot(a, b):
    return lax.dot_general(a, b, (((1,), (0,)), ((), ())), preferred_element_type=f32)


def dot_nt(a, b):
    return lax.dot_general(a, b, (((1,), (1,)), ((), ())), preferred_element_type=f32)


def dot_tn(a, b):
    return lax.dot_general(a, b, (((0,), (0,)), ((), ())), preferred_element_type=f32)


def normalize(values):
    center = values - jnp.mean(values, axis=-1, keepdims=True)
    inverse = lax.rsqrt(jnp.mean(center * center, axis=-1, keepdims=True) + epsilon)
    return center * inverse, inverse


def norm_back(upstream, normed, inverse):
    return inverse * (
        upstream
        - jnp.mean(upstream, axis=-1, keepdims=True)
        - normed * jnp.mean(upstream * normed, axis=-1, keepdims=True)
    )


def token_sum(values):
    return jnp.sum(values, axis=0, keepdims=True)


def half_masks():
    lane = lax.broadcasted_iota(jnp.int32, (SEQ, PAIR), 1)
    return lane < HD


def forward_layer(z, mod, alive, wa, wd, saved):
    def save(name, where, value):
        if saved is not None:
            saved[name][where] = value

    row = lambda i: mod[i : i + 1, :]
    normed, _ = normalize(z)
    first_in = (normed * (1.0 + row(1)) + row(0)).astype(bf16)
    parts = [dot(first_in, wa[j]).astype(bf16) for j in range(3)]
    for j in range(3):
        save("qkv", (slice(None), slice(j * D, (j + 1) * D)), parts[j])
    low_half = half_masks()
    mixed = []
    for pair in range(H // 2):
        cols = slice(pair * PAIR, (pair + 1) * PAIR)
        q, k, v = (part[:, cols] for part in parts)
        outs = []
        for e in range(2):
            mask = low_half if e == 0 else jnp.logical_not(low_half)
            q_e = jnp.where(mask, q * HD ** (-0.5), 0).astype(bf16)
            scores = dot_nt(q_e, k)
            grown = jnp.exp(scores - jnp.max(scores, axis=-1, keepdims=True))
            probs = (grown * (1.0 / jnp.sum(grown, axis=-1, keepdims=True))).astype(bf16)
            save("probs", pair * 2 + e, probs)
            outs.append(dot(probs, v))
        mixed.append(jnp.where(low_half, outs[0], outs[1]).astype(bf16))
    mixture = jnp.concatenate(mixed, axis=1)
    save("mixture", ..., mixture)
    attended = dot(mixture, wa[3])
    save("attended", ..., attended)
    middle = z + row(2) * attended
    normed_two, _ = normalize(middle)
    second_in = (normed_two * (1.0 + row(4)) + row(3)).astype(bf16)
    result = jnp.zeros((SEQ, D), f32)
    c0 = (2.0 / jnp.pi) ** 0.5
    for c in range(CHUNKS):
        cols = slice(c * D, (c + 1) * D)
        hidden = dot(second_in, wa[4 + c])
        square = hidden * hidden
        tanh = jnp.tanh(c0 * hidden * (1.0 + 0.044715 * square))
        half = 0.5 * (1.0 + tanh)
        activated = (hidden * half).astype(bf16)
        save("activated", (slice(None), cols), activated)
        if saved is not None:
            bend = 0.5 * hidden * (1.0 - tanh * tanh)
            slope = half + bend * (c0 * (1.0 + 3 * 0.044715 * square))
            save("slope", (slice(None), cols), slope.astype(bf16))
        result = result + dot(activated, wd(c))
    save("result", ..., result)
    return (middle + row(5) * result) * alive


def backward_mlp(grad_out, z, mod, alive, wa, wd, saved, pack=None):
    row = lambda i: mod[i : i + 1, :]
    attended = saved["attended"][...]
    middle = z + row(2) * attended
    normed_two, inverse_two = normalize(middle)
    grad_y = grad_out * alive
    grad_gate_m = token_sum(grad_y * saved["result"][...])
    grad_result = (row(5) * grad_y).astype(bf16)
    grad_second = jnp.zeros((SEQ, D), f32)
    if pack is not None:
        pack[:, 0:D] = (normed_two * (1.0 + row(4)) + row(3)).astype(bf16)
        pack[:, D : 2 * D] = grad_result
    for c in range(CHUNKS):
        cols = slice(c * D, (c + 1) * D)
        grad_act = dot_nt(grad_result, wd(c))
        grad_hidden = (grad_act * saved["slope"][:, cols].astype(f32)).astype(bf16)
        if pack is not None:
            pack[:, 2 * D + c * D : 2 * D + (c + 1) * D] = grad_hidden
        grad_second = grad_second + dot_nt(grad_hidden, wa[4 + c])
    grad_scale_m = token_sum(grad_second * normed_two)
    grad_shift_m = token_sum(grad_second)
    grad_middle = grad_y + norm_back(grad_second * (1.0 + row(4)), normed_two, inverse_two)
    grad_gate_a = token_sum(grad_middle * attended)
    return grad_middle, (grad_gate_a, grad_shift_m, grad_scale_m, grad_gate_m)


def backward_attention(grad_middle, z, mod, wa, saved, pack=None):
    row = lambda i: mod[i : i + 1, :]
    normed, inverse = normalize(z)
    grad_attended = (row(2) * grad_middle).astype(bf16)
    grad_mixture = dot_nt(grad_attended, wa[3]).astype(bf16)
    low_half = half_masks()
    grads = [[], [], []]
    zero = jnp.zeros((SEQ, PAIR), bf16)
    for pair in range(H // 2):
        cols = [slice(j * D + pair * PAIR, j * D + (pair + 1) * PAIR) for j in range(3)]
        q, k, v = (saved["qkv"][:, c] for c in cols)
        grad_mix = grad_mixture[:, pair * PAIR : (pair + 1) * PAIR]
        outs = []
        for e in range(2):
            mask = low_half if e == 0 else jnp.logical_not(low_half)
            probs = saved["probs"][pair * 2 + e]
            grad_probs = dot_nt(jnp.where(mask, grad_mix, zero), v)
            wide = probs.astype(f32)
            weighted = grad_probs * wide
            grad_scores = (weighted - wide * jnp.sum(weighted, axis=-1, keepdims=True)).astype(bf16)
            outs.append(
                (
                    dot(grad_scores, k) * HD ** (-0.5),
                    dot_tn(grad_scores, q) * HD ** (-0.5),
                    dot_tn(probs, grad_mix),
                )
            )
        for j in range(3):
            grads[j].append(jnp.where(low_half, outs[0][j], outs[1][j]).astype(bf16))
    grads = [jnp.concatenate(g, axis=1) for g in grads]
    grad_first = dot_nt(grads[0], wa[0]) + dot_nt(grads[1], wa[1]) + dot_nt(grads[2], wa[2])
    if pack is not None:
        pack[:, 0:D] = (normed * (1.0 + row(1)) + row(0)).astype(bf16)
        for j in range(3):
            pack[:, D + j * D : 2 * D + j * D] = grads[j]
        pack[:, 5 * D : 6 * D] = grad_attended
    grad_scale_a = token_sum(grad_first * normed)
    grad_shift_a = token_sum(grad_first)
    grad_in = grad_middle + norm_back(grad_first * (1.0 + row(1)), normed, inverse)
    return grad_in, (grad_shift_a, grad_scale_a)


SAVED = (
    ("qkv", (SEQ, 3 * D), bf16),
    ("probs", (H, SEQ, SEQ), bf16),
    ("mixture", (SEQ, D), bf16),
    ("attended", (SEQ, D), f32),
    ("activated", (SEQ, FF), bf16),
    ("slope", (SEQ, FF), bf16),
    ("result", (SEQ, D), f32),
)
NAMES = tuple(name for name, _, _ in SAVED)


def weight_copies(scalars, own, other, layer, wa, wd, sem):
    pieces = len(own)
    rows = D // pieces
    dp = scalars[0]
    mine = scalars[2] == layer

    def make(source, k):
        place = jnp.bitwise_xor(dp, k) if pieces > 1 else 0
        start = pl.multiple_of(place * rows, 16)
        first = pltpu.make_async_copy(
            source[k].at[pl.ds(0, 8)], wa.at[:, pl.ds(start, rows), :], sem.at[0, k]
        )
        second = pltpu.make_async_copy(
            source[k].at[pl.ds(8, 4)], wd.at[pl.ds(place * 4, 4)], sem.at[1, k]
        )
        return first, second

    def start():
        for source, chosen in ((own, mine), (other, jnp.logical_not(mine))):

            @pl.when(chosen)
            def _():
                for k in range(pieces):
                    for copy in make(source, k):
                        copy.start()

    def wait():
        for k in range(pieces):
            for copy in make(own, k):
                copy.wait()

    return start, wait


def down_chunk(wd_ref):
    blocks = wd_ref.shape[0]
    per = blocks // CHUNKS
    rows = wd_ref.shape[1]

    def chunk(c):
        return wd_ref[c * per : (c + 1) * per].reshape(per * rows, D)

    return chunk


def put(chosen, keep, give, value):
    @pl.when(chosen)
    def _():
        keep[...] = value

    @pl.when(jnp.logical_not(chosen))
    def _():
        give[...] = value


def weight_scratch(pieces, layers):
    rows = D // pieces
    return [
        pltpu.VMEM((layers, 8, D, D), bf16),
        pltpu.VMEM((layers, 4 * pieces, rows, D), bf16),
        pltpu.SemaphoreType.DMA((layers, 2, pieces)),
    ]


vmem = pl.BlockSpec(memory_space=pltpu.VMEM)
smem = pl.BlockSpec(memory_space=pltpu.SMEM)
hbm = pl.BlockSpec(memory_space=pl.ANY)
sent = pl.BlockSpec(memory_space=pltpu.HBM)


PACK_M, PACK_A = 10 * D, 6 * D
packs_shape = (SEQ, PACK_M + PACK_A)


def layer_weights(scalars, own, other, wa, wd, sems, order):
    handles = [
        weight_copies(scalars, own, other, layer, wa.at[layer], wd.at[layer], sems.at[layer])
        for layer in range(2)
    ]
    for layer in order:
        handles[layer][0]()
    return [handle[1] for handle in handles]


def live_factor(scalars):
    return jnp.where(scalars[3] > 0, 1.0, 0.0).astype(f32)


def first_kernel(pieces, scalars, latents, mods, *refs):
    own, other = refs[:pieces], refs[pieces : 2 * pieces]
    out, wa, wd, sems = refs[2 * pieces :]
    waits = layer_weights(scalars, own, other, wa, wd, sems, (0, 1))
    z = latents[scalars[2]]
    for layer in range(2):
        waits[layer]()
        weights = wa.at[layer], down_chunk(wd.at[layer])
        z = forward_layer(z.astype(f32), mods[layer], live_factor(scalars), *weights, None)
        z = z.astype(bf16)
    out[...] = z


def middle_kernel(pieces, scalars, latents, arriving, cots, mods, *refs):
    own, other = refs[:pieces], refs[pieces : 2 * pieces]
    rest = refs[2 * pieces :]
    act_a, keep, give, out = rest[:4]
    kept, (wa, wd, sems) = rest[4:18], rest[18:]
    saved = [dict(zip(NAMES, kept[7 * layer : 7 * layer + 7])) for layer in range(2)]
    waits = layer_weights(scalars, own, other, wa, wd, sems, (0, 1))
    weights = [(wa.at[layer], down_chunk(wd.at[layer])) for layer in range(2)]
    alive = live_factor(scalars)
    z = jnp.where(scalars[1] == 0, latents[scalars[2]], arriving[...])
    inputs = []
    for layer in range(2):
        waits[layer]()
        inputs.append(z)
        z = forward_layer(z.astype(f32), mods[layer], alive, *weights[layer], saved[layer])
        z = z.astype(bf16)
        put(scalars[2] == layer, keep, give, z)
        if layer == 0:
            act_a[...] = z
    upstream = cots[scalars[2]]
    for layer in (1, 0):
        z = inputs[layer] if layer == 0 else act_a[...]
        z = z.astype(f32)
        grad_middle, _ = backward_mlp(
            upstream.astype(f32), z, mods[layer], alive, *weights[layer], saved[layer]
        )
        grad_z, _ = backward_attention(grad_middle, z, mods[layer], wa.at[layer], saved[layer])
        upstream = grad_z.astype(bf16)
    out[...] = upstream


def last_kernel(pieces, scalars, cots, lats, grad_in, z_in, act, mods, *refs):
    own, other = refs[:pieces], refs[pieces : 2 * pieces]
    rest = refs[2 * pieces :]
    kept, rest = rest[:14], rest[14:]
    keep_z, give_z, grad_mod, keep_pack, give_pack = rest[:5]
    wa, wd, sems, packs, copy_sems, out_sems = rest[5:]
    saved = [dict(zip(NAMES, kept[7 * layer : 7 * layer + 7])) for layer in range(2)]
    pack = [packs.at[jnp.where(scalars[2] == layer, 0, 1)] for layer in range(2)]
    direct = (("activated", pl.ds(6 * D, FF)), ("mixture", pl.ds(PACK_M + 4 * D, D)))
    copies = [
        pltpu.make_async_copy(saved[layer][name], pack[layer].at[:, cols], copy_sems.at[layer, i])
        for layer in range(2)
        for i, (name, cols) in enumerate(direct)
    ]
    waits = layer_weights(scalars, own, other, wa, wd, sems, (1, 0))
    for copy in copies:
        copy.start()
    alive = live_factor(scalars)
    upstream = jnp.where(scalars[1] == 1, cots[scalars[2]], grad_in[...])
    for layer in (1, 0):
        chosen = scalars[2] == layer
        waits[layer]()
        pack_m = pack[layer].at[:, pl.ds(0, PACK_M)]
        pack_a = pack[layer].at[:, pl.ds(PACK_M, PACK_A)]
        z = act[...] if layer == 1 else jnp.where(scalars[1] == 0, lats[scalars[2]], z_in[...])
        z = z.astype(f32)
        grad_middle, four = backward_mlp(
            upstream.astype(f32),
            z,
            mods[layer],
            alive,
            wa.at[layer],
            down_chunk(wd.at[layer]),
            saved[layer],
            pack_m,
        )
        grad_z, two = backward_attention(
            grad_middle, z, mods[layer], wa.at[layer], saved[layer], pack_a
        )
        upstream = grad_z.astype(bf16)
        put(chosen, keep_z, give_z, upstream)
        grad_mod[layer] = jnp.concatenate(two + four, axis=0)
        for copy in copies[2 * layer : 2 * layer + 2]:
            copy.wait()
        for take, slot, target in (
            (chosen, 0, keep_pack),
            (jnp.logical_not(chosen), 1, give_pack),
        ):

            @pl.when(take)
            def _():
                pltpu.make_async_copy(packs.at[slot], target, out_sems.at[slot]).start()

    for slot, target in enumerate((keep_pack, give_pack)):
        pltpu.make_async_copy(packs.at[slot], target, out_sems.at[slot]).wait()


token_shape = jax.ShapeDtypeStruct((SEQ, D), bf16)
saved_shapes = [jax.ShapeDtypeStruct(shape, kind) for _, shape, kind in SAVED] * 2


def limit(mebibytes):
    return pltpu.CompilerParams(vmem_limit_bytes=mebibytes * 1024 * 1024)


def run_first(scalars, latents, mods, own, other):
    pieces = len(own)
    return pl.pallas_call(
        partial(first_kernel, pieces),
        out_shape=token_shape,
        in_specs=[smem, vmem, vmem] + [hbm] * (2 * pieces),
        out_specs=vmem,
        scratch_shapes=weight_scratch(pieces, 2),
        compiler_params=limit(12),
        name="first",
    )(scalars, latents, mods, *own, *other)


def run_middle(scalars, latents, arriving, cots, mods, own, other):
    pieces = len(own)
    out = pl.pallas_call(
        partial(middle_kernel, pieces),
        out_shape=[token_shape] * 4 + saved_shapes,
        in_specs=[smem] + [vmem] * 4 + [hbm] * (2 * pieces),
        out_specs=[vmem] * 18,
        scratch_shapes=weight_scratch(pieces, 2),
        compiler_params=limit(14),
        name="middle",
    )(scalars, latents, arriving, cots, mods, *own, *other)
    return out[:4], out[4:]


def run_last(scalars, cots, lats, grad_in, z_in, act, mods, own, other, saved):
    pieces = len(own)
    pack = jax.ShapeDtypeStruct(packs_shape, bf16)
    return pl.pallas_call(
        partial(last_kernel, pieces),
        out_shape=[token_shape] * 2 + [jax.ShapeDtypeStruct((2, 6, D), f32)] + [pack] * 2,
        in_specs=[smem] + [vmem] * 6 + [hbm] * (2 * pieces) + [vmem] * 14,
        out_specs=[vmem] * 3 + [sent] * 2,
        scratch_shapes=weight_scratch(pieces, 2)
        + [
            pltpu.VMEM((2, *packs_shape), bf16),
            pltpu.SemaphoreType.DMA((2, 2)),
            pltpu.SemaphoreType.DMA((2,)),
        ],
        compiler_params=limit(20),
        name="last",
    )(scalars, cots, lats, grad_in, z_in, act, mods, *own, *other, *saved)


def weight_grad_kernel(pieces, scalars, keep, got, *refs):
    outs, (packs, block, tall, sems, load_sems) = refs[:pieces], refs[pieces:]
    rows = D // pieces
    dp = scalars[0]
    spans = (pl.ds(PACK_M, PACK_A), pl.ds(0, 6 * D), pl.ds(6 * D, FF))
    loads = [
        [
            pltpu.make_async_copy(source.at[:, span], packs.at[i, :, span], load_sems.at[i, j])
            for i, source in enumerate((keep, got))
        ]
        for j, span in enumerate(spans)
    ]
    for pair in loads:
        for copy in pair:
            copy.start()

    def arrived(j):
        for copy in loads[j]:
            copy.wait()

    def send(stage, k):
        place = jnp.bitwise_xor(dp, k) if pieces > 1 else 0
        if stage == 0:
            start = pl.multiple_of(place * rows, 16)
            source, target = block.at[:, pl.ds(start, rows), :], outs[k].at[pl.ds(0, 8)]
        else:
            source, target = tall.at[pl.ds(place * 4, 4)], outs[k].at[pl.ds(8, 4)]
        return pltpu.make_async_copy(source, target, sems.at[stage, k])

    def product(a, b, wide):
        left, right = slice(a * D, (a + 1) * D), slice(b * D, (b + wide) * D)
        return dot_tn(
            packs[:, :, left].reshape(2 * SEQ, (left.stop - left.start)),
            packs[:, :, right].reshape(2 * SEQ, (right.stop - right.start)),
        ).astype(bf16)

    arrived(0)
    for base, a, b, wide in ((0, 10, 11, 3), (3, 14, 15, 1), (4, 0, 2, 2), (6, 0, 4, 2)):
        if base == 4:
            arrived(1)
        result = product(a, b, wide)
        for j in range(wide):
            block[base + j] = result[:, j * D : (j + 1) * D]
    for k in range(pieces):
        send(0, k).start()
    per = D // rows
    arrived(2)
    for c in range(CHUNKS):
        tall[c * per : (c + 1) * per] = product(6 + c, 1, 1).reshape(per, rows, D)
    for k in range(pieces):
        send(1, k).start()
    for k in range(pieces):
        send(0, k).wait()
        send(1, k).wait()


def run_weight_grad(pieces, scalars, keep, got):
    rows = D // pieces
    return pl.pallas_call(
        partial(weight_grad_kernel, pieces),
        out_shape=[jax.ShapeDtypeStruct((BLOCKS, rows, D), bf16)] * pieces,
        in_specs=[smem] + [hbm] * 2,
        out_specs=[sent] * pieces,
        scratch_shapes=[
            pltpu.VMEM((2, *packs_shape), bf16),
            pltpu.VMEM((8, D, D), bf16),
            pltpu.VMEM((FF // rows, rows, D), bf16),
            pltpu.SemaphoreType.DMA((2, pieces)),
            pltpu.SemaphoreType.DMA((2, 3)),
        ],
        compiler_params=limit(58),
        name="weight_grad",
    )(scalars, keep, got)


def total_kernel(*refs):
    parts, (qkv, out, up, down) = refs[:5], refs[5:]
    rows = out.shape[0]

    def total(j):
        value = parts[0][j].astype(f32)
        for part in parts[1:]:
            value = value + part[j].astype(f32)
        return value

    for j in range(3):
        qkv[:, j * D : (j + 1) * D] = total(j)
    out[...] = total(3)
    for c in range(CHUNKS):
        up[:, c * D : (c + 1) * D] = total(4 + c)
        down[c * rows : (c + 1) * rows, :] = total(8 + c)


def run_total(*parts):
    rows = parts[0].shape[1]
    shapes = ((rows, 3 * D), (rows, D), (rows, FF), (CHUNKS * rows, D))
    return pl.pallas_call(
        total_kernel,
        out_shape=[jax.ShapeDtypeStruct(shape, f32) for shape in shapes],
        in_specs=[vmem] * 5,
        out_specs=[vmem] * 4,
        compiler_params=limit(4),
        name="total",
    )(*parts)


def joined(first, second):
    return (first.astype(f32) + second.astype(f32)).astype(bf16)


def swap(value, axis, bit):
    count = lax.axis_size(axis)
    return lax.ppermute(value, axis, [(i, i ^ bit) for i in range(count)])


def one_way(value, axis, source, target):
    return lax.ppermute(value, axis, [(source, target)])


def exchange(value, axes):
    return lax.all_to_all(value, axes, split_axis=0, concat_axis=0, tiled=True)


def spread(value, axes):
    return exchange(jnp.broadcast_to(value[None], (lax.axis_size(axes), *value.shape)), axes)


def local(
    latents_in,
    cotangent,
    labels,
    timesteps,
    counts,
    label_table,
    time_table,
    adaptive_norm_weight,
    adaptive_norm_bias,
    query_key_value_weight,
    attention_output_weight,
    up_weight,
    down_weight,
):
    dp_count = lax.axis_size("dp")
    dp, x, core = (lax.axis_index(name) for name in ("dp", "x", "core"))
    rows = D // dp_count
    small = dp_count == 8
    latents = latents_in[:, 0]
    cotangents = cotangent[:, 0]
    live = jnp.where(core == 0, counts[0, 0], counts[1, 0])
    scalars = jnp.stack([dp, x, core, live]).astype(jnp.int32)

    ids = spread(jnp.concatenate([labels[:, 0], timesteps[:, 0]]), "dp")
    ids = ids.reshape(dp_count, 2, MICRO).transpose(1, 2, 0).reshape(2, MICRO * dp_count)

    if small:
        shard = jnp.concatenate(
            [
                query_key_value_weight[0].reshape(rows, 3, D).transpose(1, 0, 2),
                attention_output_weight[0][None],
                up_weight[0].reshape(rows, CHUNKS, D).transpose(1, 0, 2),
                down_weight[0].reshape(CHUNKS, rows, D),
            ],
            axis=0,
        )
        own = {0: shard, 2: swap(shard, "dp", 2), 4: swap(shard, "dp", 4), 1: swap(shard, "dp", 1)}
        shard, ids, own[1], own[2], own[4] = lax.optimization_barrier(
            (shard, ids, own[1], own[2], own[4])
        )
        own[6] = swap(shard, "dp", 6)
        own[3], own[5] = swap(own[2], "dp", 1), swap(own[4], "dp", 1)
    else:
        blocks = jnp.concatenate(
            [
                query_key_value_weight[0].reshape(rows, 3, D).transpose(1, 0, 2),
                attention_output_weight[0][None],
                up_weight[0].reshape(rows, CHUNKS, D).transpose(1, 0, 2),
            ],
            axis=0,
        )
        own = [
            jnp.concatenate(
                [
                    lax.all_gather(blocks, "dp", axis=1, tiled=True),
                    lax.all_gather(down_weight[0], "dp", axis=0, tiled=True).reshape(CHUNKS, D, D),
                ],
                axis=0,
            )
        ]

    condition = label_table[ids[0]] + time_table[ids[1]]
    condition = lax.dynamic_slice_in_dim(condition, dp * rows, rows, axis=1)
    cond_act = jax.nn.silu(condition).astype(bf16)
    ada = adaptive_norm_weight[0]
    width = 6 * D // dp_count
    bias = lax.dynamic_update_slice_in_dim(
        jnp.zeros((6 * D,), f32), adaptive_norm_bias[0].astype(f32), dp * width, 0
    )
    linear = jnp.dot(cond_act, ada, preferred_element_type=f32) + bias
    linear = exchange(linear, ("core", "dp"))
    mods = jnp.sum(linear.reshape(2, dp_count, 6 * D), axis=1).reshape(2, 6, D)
    if small:
        own[6], mods, own[3], own[5] = lax.optimization_barrier((own[6], mods, own[3], own[5]))
        own[7] = swap(own[6], "dp", 1)
        own = [own[k] for k in range(8)]
    pieces = len(own)
    other = [swap(piece, "core", 1) for piece in own]

    leaving = run_first(scalars, latents, mods, own, other)
    arriving = one_way(leaving, "x", 0, 1)
    (act_a, keep_act, give_act, grad_out), saved = run_middle(
        scalars, latents, arriving, cotangents, mods, own, other
    )
    grad_in = one_way(grad_out, "x", 1, 0)
    keep_z, give_z, grad_mod, keep_pack, give_pack = run_last(
        scalars, cotangents, latents, grad_in, arriving, act_a, mods, own, other, saved
    )

    def both_micros(mine, theirs):
        return jnp.where(core == 0, jnp.stack([mine, theirs]), jnp.stack([theirs, mine]))

    got_pack = swap(give_pack, "core", 1)
    grad_mod = jnp.broadcast_to(grad_mod.reshape(2, 1, 6 * D), (2, dp_count, 6 * D))
    grad_mod = exchange(grad_mod.reshape(2 * dp_count, 6 * D), ("core", "dp"))
    parts = list(run_weight_grad(pieces, scalars, keep_pack, got_pack))
    across = {}
    if small:
        across = {k: swap(parts[2 * k + 1], "dp", 1) for k in (3, 2, 1, 0)}
        grad_mod, across[3] = lax.optimization_barrier((grad_mod, across[3]))
    grad_mod_low = grad_mod.astype(bf16)
    _, silu_pull = jax.vjp(jax.nn.silu, condition)
    grad_cond = silu_pull(
        lax.dot_general(grad_mod_low, ada, (((1,), (1,)), ((), ())), preferred_element_type=f32)
    )[0]
    if small:
        grad_cond, across[2] = lax.optimization_barrier((grad_cond, across[2]))
        far = [swap(joined(parts[2 * k], across[k]), "dp", 2 * k) for k in (3, 2, 1)]
        weight_grads = run_total(*far, parts[0], across[0])
    else:
        square = lax.psum_scatter(
            parts[0][:8].astype(f32), "dp", scatter_dimension=1, tiled=True
        )
        tall = lax.psum_scatter(
            parts[0][8:].astype(f32).reshape(FF, D), "dp", scatter_dimension=0, tiled=True
        )
        weight_grads = (
            square[0:3].transpose(1, 0, 2).reshape(rows, 3 * D),
            square[3],
            square[4:8].transpose(1, 0, 2).reshape(rows, FF),
            tall,
        )
    acts = both_micros(keep_act, swap(give_act, "core", 1))
    act_grads = both_micros(keep_z, swap(give_z, "core", 1))

    grad_w_ada = jnp.dot(cond_act.T, grad_mod_low, preferred_element_type=f32)
    grad_b_ada = lax.dynamic_slice_in_dim(jnp.sum(grad_mod, axis=0), dp * width, width)
    table_rows = spread(grad_cond, ("x", "core", "dp"))
    table_rows = jnp.sum(table_rows.reshape(4, dp_count, MICRO * dp_count, rows), axis=0)
    table_rows = table_rows.transpose(1, 0, 2).reshape(MICRO * dp_count, D)
    share = CLASSES // (4 * dp_count)
    base = ((x * 2 + core) * dp_count + dp) * share
    targets = base + jnp.arange(share, dtype=jnp.int32)
    label_hot = (targets[:, None] == ids[0][None, :]).astype(f32)
    time_hot = (targets[:, None] == ids[1][None, :]).astype(f32)
    label_part = jnp.dot(label_hot, table_rows, precision=highest)
    time_part = jnp.dot(time_hot, table_rows, precision=highest)

    grad_w_qkv, grad_w_out, grad_w_up, grad_w_down = weight_grads

    return (
        acts[None, :, None],
        act_grads[None, :, None],
        grad_w_ada[None],
        grad_b_ada[None],
        grad_w_qkv[None],
        grad_w_out[None],
        grad_w_up[None],
        grad_w_down[None],
        label_part,
        time_part,
    )


def solution(mesh):
    sections, dp_count = mesh.devices.shape
    grid = Mesh(mesh.devices.reshape(2, sections // 2, dp_count), ("x", "core", "dp"))
    section = ("x", "core")
    return jax.shard_map(
        local,
        mesh=grid,
        in_specs=(
            P(None, "dp", None, None),
            P(None, "dp", None, None),
            P(None, "dp"),
            P(None, "dp"),
            P(None, "dp"),
            P(),
            P(),
            P(section, "dp", None),
            P(section, "dp"),
            P(section, "dp", None),
            P(section, "dp", None),
            P(section, "dp", None),
            P(section, "dp", None),
        ),
        out_specs=(
            P(section, None, "dp", None, None),
            P(section, None, "dp", None, None),
            P(section, "dp", None),
            P(section, "dp"),
            P(section, "dp", None),
            P(section, "dp", None),
            P(section, "dp", None),
            P(section, "dp", None),
            P(("x", "core", "dp"), None),
            P(("x", "core", "dp"), None),
        ),
        check_vma=False,
    )
```
